512 devices in a mesh: dp: 64 (over z_lo, y, core), split: 8 (over x, z_hi).
Axes of the slice: x: 4, y: 8, z: 8 (z_hi: 2, z_lo: 4; z = z_hi * 4 + z_lo), core: 2. Of those that a mesh axis runs over, the one named last changes fastest.
Arguments:
- image: float32 [14336, 768], P('dp'), may hold values from -0.5 to 0.5, as said below
- text: float32 [14336, 768], P('dp'), may hold values from -0.5 to 0.5, as said below
- log_temp: float32 [1], replicated, may hold values from 1.6 to 2.4
- bias: float32 [1], replicated, may hold values from -3 to -1.5
Outputs:
- loss: float32 [], replicated
- grad_image: float32 [14336, 768], P(('dp', 'split'))
- grad_text: float32 [14336, 768], P(('dp', 'split'))
The draws below stay inside these ranges and needn't reach their ends.
Inputs may be any that keep to these rules, and one draw needn't show every extreme that they name: Entries of the image embeddings are of order 768 ** -0.5. Entries of the text embeddings are of order 768 ** -0.5.
All inputs are finite; a program needn't handle non-finite values.
Results may differ from the reference program's by a relative error of at most 0.0003.
Values sent between devices are 32-bit elements; how exact they have to be, the bound alone decides.
A program may use at most 64 MiB of HBM per device.

```python
import jax
import jax.numpy as jnp
from jax import lax

D = 768
ROWS = 224
N = 14336
N_DP = 64


def sign_table(key, shape):
    signs = jax.random.bernoulli(key, 0.5, shape).astype(jnp.float32)
    return (2.0 * signs - 1.0) / jnp.sqrt(jnp.float32(D))


def shared_parts(key):
    table = sign_table(jax.random.fold_in(key, 7), (16, D))
    member_ids = jax.random.randint(jax.random.fold_in(key, 5), (N,), 0, 16)
    return jnp.take(table, member_ids, axis=0)


def noise_normal(key):
    return jnp.clip(0.036 * jax.random.normal(key, (N, D), jnp.float32), -0.216, 0.216)


def draw_image(key, part):
    cluster = shared_parts(key)
    key = jax.random.fold_in(key, 11)
    noise = noise_normal(key)
    top = 0.5
    heading = cluster
    ramp = top * jnp.arange(N, dtype=jnp.float32) / jnp.float32(N - 1)
    return noise + ramp[:, None] * heading


def draw_text(key, part):
    cluster = shared_parts(key)
    key = jax.random.fold_in(key, 23)
    noise = noise_normal(key)
    heading = cluster
    return noise + heading


def setup_inputs(seed: int = 0) -> dict:
    streams_of = jax.random.split(jax.random.key(seed), 5)
    image = draw_image(jax.random.fold_in(streams_of[4], 71), 0)
    text = draw_text(jax.random.fold_in(streams_of[4], 71), 0)
    log_temp = jnp.clip(jax.random.uniform(streams_of[2], (1,), jnp.float32, 1.6, 2.4), 1.6, 2.4)
    bias = jnp.clip(jax.random.uniform(streams_of[3], (1,), jnp.float32, -3.0, -1.5), -3.0, -1.5)
    return dict(image=image, text=text, log_temp=log_temp, bias=bias)


EPS = 1e-06

def normalize(values):
    inverse = lax.rsqrt(lax.optimization_barrier(jnp.sum(values * values, axis=-1, keepdims=True)) + EPS)
    return (values * inverse, inverse)

def reference(image, text, log_temp, bias):
    x_hat, inv_x = normalize(image)
    y_hat, inv_y = normalize(text)
    scale = jnp.exp(log_temp[0])
    offset = bias[0]
    columns = jnp.arange(N, dtype=jnp.int32)

    def one_block(carry, index):
        total, g_y = carry
        start = (index * ROWS).astype(jnp.int32)
        rows_hat = lax.dynamic_slice_in_dim(x_hat, start, ROWS, 0)
        logits = scale * jnp.dot(rows_hat, y_hat.T, precision=lax.Precision.HIGHEST) + offset
        row_ids = start + jnp.arange(ROWS, dtype=jnp.int32)
        label = (row_ids[:, None] == columns[None, :]).astype(jnp.float32)
        total = total + jnp.sum(jax.nn.softplus(logits - 2.0 * label * logits))
        delta = jax.nn.sigmoid(logits) - label
        g_x = scale * jnp.dot(delta, y_hat, precision=lax.Precision.HIGHEST)
        g_y = g_y + scale * jnp.dot(delta.T, rows_hat, precision=lax.Precision.HIGHEST)
        return ((total, g_y), g_x)
    start_carry = (jnp.zeros((), jnp.float32), jnp.zeros((N, D), jnp.float32))
    (total, g_y), g_blocks = lax.scan(one_block, start_carry, jnp.arange(N_DP, dtype=jnp.int32))
    g_x = g_blocks.reshape(N, D)
    grad_image = inv_x * (g_x - x_hat * lax.optimization_barrier(jnp.sum(x_hat * g_x, axis=-1, keepdims=True)))
    grad_text = inv_y * (g_y - y_hat * lax.optimization_barrier(jnp.sum(y_hat * g_y, axis=-1, keepdims=True)))
    loss = total / (jnp.float32(N) * jnp.float32(N))
    return (loss, grad_image, grad_text)
```

```python
import functools

import jax
import jax.numpy as jnp
from jax import lax
from jax.experimental import pallas as pl
from jax.experimental.pallas import tpu as pltpu
from jax.sharding import PartitionSpec as P

EPS = 1e-06
MESH = pl.DeviceIdType.MESH
D = 768
NX, NY, NZ, NL = 4, 8, 8, 4
SHARE = 28
PAD = 32
BLOCK = 224
TEXT = 56
S = NX * NL * PAD
T = 2 * NY * TEXT
HALF = D // 2
NC = 3
CC = D // NC
TILE = 128
F32 = jnp.float32
BF16 = jnp.bfloat16


def split_bf16(v):
    hi = v.astype(BF16)
    return hi, (v - hi.astype(F32)).astype(BF16)


def dot(a, b, ca, cb):
    return lax.dot_general(a, b, (((ca,), (cb,)), ((), ())), preferred_element_type=F32)


def kernel(
    img, txt, lt_ref, bias_ref,
    loss_o, gi_o, gt_o,
    xh, invx, xs, ys, xb_hi, xb_lo, yb_hi, yb_lo, d_hi, d_lo,
    gy, gy_in, rs_in, gz, gz_in, gxs, xr, zs, zr, lacc, lc, lx, ly, lz, lm,
    z_ss, z_rs, ag_ss, ag_rs, co_ss, co_rs, gc_ss, gc_rs, rs_ss, rs_rs,
    h_ss, h_rs, x_ss, x_rs, q_ss, q_rs, lc_ss, lc_rs, lx_ss, lx_rs, ly_ss, ly_rs, lz_ss, lz_rs,
):
    dp = lax.axis_index("dp")
    split = lax.axis_index("split")
    k = lax.rem(dp, 2)
    y = lax.rem(lax.div(dp, 2), NY)
    zl = lax.div(dp, 2 * NY)
    x = lax.div(split, 2)
    zh = lax.rem(split, 2)
    z = zh * NL + zl

    def dev(x_, y_, z_, k_):
        return (lax.rem(z_, NL) * (2 * NY) + y_ * 2 + k_, x_ * 2 + lax.div(z_, NL))

    def at_x(d):
        return dev(lax.rem(x + d, NX), y, z, k)

    def at_y(d):
        return dev(x, lax.rem(y + d, NY), z, k)

    def at_z(d):
        return dev(x, y, lax.rem(z + d, NZ), k)

    other = dev(x, y, z, 1 - k)

    def at_line(r):
        return dev(x, y, zh * NL + lax.rem(zl + r, NL), k)

    def rcopy(src, dst, ss, rs, to):
        return pltpu.make_async_remote_copy(src, dst, ss, rs, device_id=to, device_id_type=MESH)

    barrier = pltpu.get_barrier_semaphore()
    partners = [at_x(d) for d in range(1, NX)] + [at_y(d) for d in range(1, NY)]
    partners += [at_z(d) for d in range(1, NZ)] + [other]
    for to in partners:
        pl.semaphore_signal(barrier, inc=1, device_id=to, device_id_type=MESH)

    for s in range(2 * NX):
        v = img[SHARE * s : SHARE * (s + 1), :]
        inv = lax.rsqrt(jnp.sum(v * v, axis=-1, keepdims=True) + EPS)
        xh[s % 2, s // 2] = v * inv
        invx[s % 2, s // 2] = jnp.broadcast_to(inv, (SHARE, 128))
    v = txt[pl.ds(pl.multiple_of(x * TEXT, 8), TEXT), :]
    inv_y = lax.rsqrt(jnp.sum(v * v, axis=-1, keepdims=True) + EPS)
    ys[0:TEXT, :] = v * inv_y

    pl.semaphore_wait(barrier, len(partners))

    def trow(kk, dy):
        return pl.ds(kk * NY * TEXT + dy * TEXT, TEXT)

    def cols(h):
        return pl.ds(h * HALF, HALF)

    def ag(h, right, s):
        if right:
            src, dst, to = (NY - (s - 1)) % NY, NY - s, at_y(1)
        else:
            src, dst, to = s - 1, s, at_y(NY - 1)
        i = h * 8 + (0 if right else 4) + s - 1
        return rcopy(ys.at[trow(0, src), cols(h)], ys.at[trow(0, dst), cols(h)], ag_ss.at[i], ag_rs.at[i], to)

    def core_copy(dy, h):
        i = dy * 2 + h
        return rcopy(ys.at[trow(0, dy), cols(h)], ys.at[trow(1, dy), cols(h)], co_ss.at[i], co_rs.at[i], other)

    def steps(h, right):
        return NY // 2 if right == (h == 0) else NY // 2 - 1

    order = [(h, right) for h in range(2) for right in (True, False)]
    for h, right in order:
        ag(h, right, 1).start()

    def zcopy(d):
        there = lax.div(lax.rem(z + d, NZ), NL)
        if d == 1:
            return rcopy(xh.at[there], xs.at[2], z_ss.at[0], z_rs.at[0], at_z(1))
        if d == NZ - 1:
            return rcopy(xh.at[there], xs.at[0], z_ss.at[1], z_rs.at[1], at_z(NZ - 1))
        half = 0 if d == 2 else 1
        part = pl.ds(half * 2, 2)
        return rcopy(xh.at[there, part], xs.at[1, part], z_ss.at[2 + half], z_rs.at[2 + half], at_z(d))

    zcopies = [zcopy(d) for d in (1, NZ - 1, 2, NZ - 2)]
    for c in zcopies:
        c.start()
    core_copies = []
    for h in range(2):
        c = core_copy(0, h)
        c.start()
        core_copies.append(c)

    xb_hi[...] = jnp.zeros_like(xb_hi)
    xb_lo[...] = jnp.zeros_like(xb_lo)

    def put(r, block):
        for j in range(NX):
            hi, lo = split_bf16(block(j))
            row = (j * NL + r) * PAD
            xb_hi[row : row + SHARE, :] = hi
            xb_lo[row : row + SHARE, :] = lo

    put(0, lambda j: xh[zh, j])

    for s in range(1, NY // 2 + 1):
        for h, right in order:
            if s <= steps(h, right):
                ag(h, right, s).wait_recv()
                if s < steps(h, right):
                    ag(h, right, s + 1).start()
                c = core_copy(NY - s if right else s, h)
                c.start()
                core_copies.append(c)
    for c in zcopies:
        c.wait()
    for r in range(1, NL):
        put(r, lambda j: xs[r - 1, j])
    for c in core_copies:
        c.wait()
    for h, right in order:
        for s in range(1, steps(h, right) + 1):
            ag(h, right, s).wait_send()

    scale = jnp.exp(jnp.full((1, S), lt_ref[0], F32))
    offset = bias_ref[0]
    lacc[...] = jnp.zeros_like(lacc)

    def cast_tile(i, carry):
        rows = pl.ds(pl.multiple_of(i * TILE, TILE), TILE)
        hi, lo = split_bf16(ys[rows, :])
        yb_hi[rows, :] = hi
        yb_lo[rows, :] = lo
        return carry

    lax.fori_loop(0, T // TILE, cast_tile, 0)

    def pair_tile(i, carry):
        rows = pl.ds(pl.multiple_of(i * TILE, TILE), TILE)
        yh, yl = yb_hi[rows, :], yb_lo[rows, :]
        prod = dot(yh, xb_hi[...], 1, 1) + (dot(yl, xb_hi[...], 1, 1) + dot(yh, xb_lo[...], 1, 1))
        logits = scale * prod + offset
        u = jnp.exp(-jnp.abs(logits))
        w = 1.0 + u
        r = 1.0 / w
        sp = jnp.maximum(logits, 0.0) + (jnp.log(w) + (u - (w - 1.0)) * r)
        sig = jnp.where(logits >= 0.0, r, u * r)
        lacc[...] += jnp.sum(sp.reshape(TILE // 8, 8, S), axis=0)
        hi, lo = split_bf16(sig)
        gy[rows, :] = dot(hi, xb_hi[...], 1, 0) + (dot(lo, xb_hi[...], 1, 0) + dot(hi, xb_lo[...], 1, 0))
        hi, lo = split_bf16(sig.T)
        d_hi[:, rows] = hi
        d_lo[:, rows] = lo
        return carry

    lax.fori_loop(0, T // TILE, pair_tile, 0)

    def gcopy(dy):
        return rcopy(gy.at[trow(1, dy), :], gy_in.at[pl.ds(dy * TEXT, TEXT), :], gc_ss.at[dy], gc_rs.at[dy], other)

    far_first = (4, 3, 5, 2, 6, 1, 7, 0)
    for dy in far_first:
        gcopy(dy).start()

    x_own = xh[zh, x]
    y_all = ys[0:TEXT, :]
    y_own = jnp.where(zh == 0, y_all[0:SHARE, :], y_all[SHARE:TEXT, :])
    iy_own = jnp.where(zh == 0, inv_y[0:SHARE, :], inv_y[SHARE:TEXT, :])
    scale1 = scale[:, 0:1]
    lane = lax.broadcasted_iota(jnp.int32, (8, S), 1)
    pairs = jnp.sum(jnp.where(lax.rem(lane, PAD) < SHARE, lacc[...], 0.0))
    same = jnp.sum(jnp.sum(x_own * y_own, axis=-1, keepdims=True) * scale1 + offset)
    lc[k] = jnp.full((8, 128), pairs - same, F32)

    def lsend(buf, me, ss, rs, to, n):
        copies = [rcopy(buf.at[me], buf.at[me], ss.at[d - 1], rs.at[d - 1], to(d)) for d in range(1, n)]
        for c in copies:
            c.start()
        return copies

    def lsum(buf, copies, n):
        for c in copies:
            c.wait()
        out = buf[0]
        for i in range(1, n):
            out = out + buf[i]
        return out

    lcopies = lsend(lc, k, lc_ss, lc_rs, lambda d: other, 2)

    def xcopy(c, d):
        i = c * 3 + d - 1
        return rcopy(gxs.at[c, lax.rem(x + d, NX)], xr.at[c, d - 1], x_ss.at[i], x_rs.at[i], at_x(d))

    def image_sums(c):
        yh, yl = yb_hi[:, c * CC : (c + 1) * CC], yb_lo[:, c * CC : (c + 1) * CC]

        def one(j, carry):
            rows = pl.ds(pl.multiple_of(j * TILE, TILE), TILE)
            dh, dl = d_hi[rows, :], d_lo[rows, :]
            g = dot(dh, yh, 1, 0) + (dot(dl, yh, 1, 0) + dot(dh, yl, 1, 0))
            for r in range(NL):
                gxs[c, j, r] = g[r * PAD : r * PAD + SHARE, :]
            return carry

        lax.fori_loop(0, NX, one, 0)
        for d in range(1, NX):
            xcopy(c, d).start()

    def rs(h, right, s):
        n = steps(h, right)
        dist = n - s + 1
        dy = dist if right else NY - dist
        i = h * 8 + (0 if right else 4) + s - 1
        return rcopy(
            gy.at[trow(0, dy), cols(h)], rs_in.at[i], rs_ss.at[i], rs_rs.at[i], at_y(1 if right else NY - 1)
        )

    image_sums(0)
    for dy in far_first:
        gcopy(dy).wait()
        rows = pl.ds(dy * TEXT, TEXT)
        gy[rows, :] = gy[rows, :] + gy_in[rows, :]
        for h, right in order:
            n = steps(h, right)
            if dy == (n if right else NY - n):
                rs(h, right, 1).start()
    image_sums(1)
    image_sums(2)
    lx[x] = lsum(lc, lcopies, 2)
    lcopies = lsend(lx, x, lx_ss, lx_rs, at_x, NX)

    def qcopy(c, r):
        i = c * 3 + r - 1
        return rcopy(zs.at[c, r], zr.at[c, r - 1], q_ss.at[i], q_rs.at[i], at_line(r))

    def x_done(c):
        for d in range(1, NX):
            xcopy(c, d).wait()
        zs[c] = gxs[c, x] + xr[c, 0] + xr[c, 1] + xr[c, 2]
        for r in range(1, NL):
            qcopy(c, r).start()

    def rs_step(s):
        for h, right in order:
            n = steps(h, right)
            if s <= n:
                rs(h, right, s).wait_recv()
                dist = n - s
                dy = 0 if dist == 0 else (dist if right else NY - dist)
                i = h * 8 + (0 if right else 4) + s - 1
                gy[dy * TEXT : (dy + 1) * TEXT, h * HALF : (h + 1) * HALF] += rs_in[i]
                if s < n:
                    rs(h, right, s + 1).start()

    rs_step(1)
    ly[y] = lsum(lx, lcopies, NX)
    lcopies = lsend(ly, y, ly_ss, ly_rs, at_y, NY)
    x_done(0)
    rs_step(2)
    lz[z] = lsum(ly, lcopies, NY)
    lcopies = lsend(lz, z, lz_ss, lz_rs, at_z, NZ)
    x_done(1)
    rs_step(3)
    x_done(2)
    rs_step(4)
    gz[0] = gy[0:SHARE, :]
    gz[1] = gy[SHARE:TEXT, :]
    hcopy = rcopy(gz.at[1 - zh], gz_in, h_ss, h_rs, at_z(NL))
    hcopy.start()
    loss_o[...] = lsum(lz, lcopies, NZ) * (1.0 / float(BLOCK * 2 * NY * NL) ** 2)

    for c in range(NC):
        for r in range(1, NL):
            qcopy(c, r).wait()
        lm[:, c * CC : (c + 1) * CC] = zs[c, 0] + zr[c, 0] + zr[c, 1] + zr[c, 2]
    g = scale1 * (lm[...] - y_own)
    gi_o[...] = invx[zh, x][:, 0:1] * (g - x_own * jnp.sum(x_own * g, axis=-1, keepdims=True))

    hcopy.wait()
    g = scale1 * (gz[zh] + gz_in[...] - x_own)
    gt_o[...] = iy_own * (g - y_own * jnp.sum(y_own * g, axis=-1, keepdims=True))

    for h, right in order:
        for s in range(1, steps(h, right) + 1):
            rs(h, right, s).wait_send()


def local(image, text, log_temp, bias):
    vmem = pl.BlockSpec(memory_space=pltpu.VMEM)
    smem = pl.BlockSpec(memory_space=pltpu.SMEM)
    dma = pltpu.SemaphoreType.DMA
    scratch = [
        pltpu.VMEM((2, NX, SHARE, D), F32),
        pltpu.VMEM((2, NX, SHARE, 128), F32),
        pltpu.VMEM((NL - 1, NX, SHARE, D), F32),
        pltpu.VMEM((T, D), F32),
        pltpu.VMEM((S, D), BF16),
        pltpu.VMEM((S, D), BF16),
        pltpu.VMEM((T, D), BF16),
        pltpu.VMEM((T, D), BF16),
        pltpu.VMEM((S, T), BF16),
        pltpu.VMEM((S, T), BF16),
        pltpu.VMEM((T, D), F32),
        pltpu.VMEM((T // 2, D), F32),
        pltpu.VMEM((16, TEXT, HALF), F32),
        pltpu.VMEM((2, SHARE, D), F32),
        pltpu.VMEM((SHARE, D), F32),
        pltpu.VMEM((NC, NX, NL, SHARE, CC), F32),
        pltpu.VMEM((NC, NX - 1, NL, SHARE, CC), F32),
        pltpu.VMEM((NC, NL, SHARE, CC), F32),
        pltpu.VMEM((NC, NL - 1, SHARE, CC), F32),
        pltpu.VMEM((8, S), F32),
        pltpu.VMEM((2, 8, 128), F32),
        pltpu.VMEM((NX, 8, 128), F32),
        pltpu.VMEM((NY, 8, 128), F32),
        pltpu.VMEM((NZ, 8, 128), F32),
        pltpu.VMEM((SHARE, D), F32),
    ]
    for n in (4, 16, 16, 8, 16):
        scratch += [dma((n,)), dma((n,))]
    scratch += [dma, dma]
    for n in (3 * NC, 3 * NC, 1, NX - 1, NY - 1, NZ - 1):
        scratch += [dma((n,)), dma((n,))]
    loss, gi, gt = pl.pallas_call(
        kernel,
        out_shape=(
            jax.ShapeDtypeStruct((8, 128), F32),
            jax.ShapeDtypeStruct((SHARE, D), F32),
            jax.ShapeDtypeStruct((SHARE, D), F32),
        ),
        in_specs=[vmem, vmem, smem, smem],
        out_specs=(vmem, vmem, vmem),
        scratch_shapes=scratch,
        compiler_params=pltpu.CompilerParams(
            collective_id=0, has_side_effects=True, vmem_limit_bytes=48 << 20
        ),
    )(image, text, log_temp, bias)
    return loss[0, 0], gi, gt


def solution(mesh):
    in_specs = (P("dp", None), P("dp", None), P(), P())
    out_specs = (P(), P(("dp", "split"), None), P(("dp", "split"), None))
    return jax.shard_map(local, mesh=mesh, in_specs=in_specs, out_specs=out_specs, check_vma=False)
```

```python
import jax
import jax.numpy as jnp
from jax import lax
from jax.experimental import pallas as pl
from jax.experimental.pallas import tpu as pltpu
from jax.sharding import PartitionSpec as P

EPS = 1e-06
MESH = pl.DeviceIdType.MESH
D = 768
NX, NY, NZ, NL = 4, 8, 8, 4
N = 14336
SHARE = 28
BLOCK = 224
TEXT = 56
S = 4 * BLOCK
T = NY * TEXT
HALF = D // 2
NC = 3
CC = D // NC
TT = T // 2
F32 = jnp.float32
BF16 = jnp.bfloat16
SLOT = {1: 0, 7: 1, 2: 2, 6: 3, 3: 4, 5: 5, 0: 6, 4: 7}


def split_bf16(v):
    hi = v.astype(BF16)
    return hi, (v - hi.astype(F32)).astype(BF16)


def dot3(ah, al, bh, bl, ca, cb):
    def one(a, b):
        return lax.dot_general(a, b, (((ca,), (cb,)), ((), ())), preferred_element_type=F32)

    return one(ah, bh) + one(al, bh) + one(ah, bl)


def unit_rows(v):
    inv = lax.rsqrt(jnp.sum(v * v, axis=-1, keepdims=True) + EPS)
    return v * inv, inv


def kernel(
    img_hbm, txt_hbm, lt_ref, bias_ref,
    loss_o, gi_o, gt_o,
    img, txt, xo, yo, xs, ys, xb_hi, xb_lo, yb_hi, yb_lo, d_hi, d_lo,
    gy, ge_in, gf_in, rs_in, gz, gz_in, gt, gxs, gc_in, xa_in, xf_in, zs, zr, gx, lacc, lc, lx, ly, lz,
    in_s, e_ss, e_rs, ag_ss, ag_rs, ic_ss, ic_rs, iz_ss, iz_rs, ix_ss, ix_rs,
    ge_ss, ge_rs, rs_ss, rs_rs, gc_ss, gc_rs, xa_ss, xa_rs, xf_ss, xf_rs, q_ss, q_rs, h_ss, h_rs,
    lc_ss, lc_rs, lx_ss, lx_rs, ly_ss, ly_rs, lz_ss, lz_rs,
):
    dp = lax.axis_index("dp")
    split = lax.axis_index("split")
    k = lax.rem(dp, 2)
    y = lax.rem(lax.div(dp, 2), NY)
    zl = lax.div(dp, 2 * NY)
    x = lax.div(split, 2)
    zh = lax.rem(split, 2)
    z = zh * NL + zl
    odd = lax.rem(z, 2)
    zp = z + 1 - 2 * odd
    zq = lax.rem(z + 7 - 6 * odd, NZ)
    inner = jnp.where(jnp.logical_and(z >= 3, z <= 6), 1, 0)
    own = k == lax.rem(odd + inner, 2)
    guest = jnp.logical_not(own)

    def dev(x_, y_, z_, k_):
        return (lax.rem(z_, NL) * (2 * NY) + y_ * 2 + k_, x_ * 2 + lax.div(z_, NL))

    def at_x(d):
        return dev(lax.rem(x + d, NX), y, z, k)

    def at_y(d):
        return dev(x, lax.rem(y + d, NY), z, k)

    def at_z(z_):
        return dev(x, y, lax.rem(z_, NZ), k)

    other = dev(x, y, z, 1 - k)

    def rcopy(src, dst, ss, rs, to):
        return pltpu.make_async_remote_copy(src, dst, ss, rs, device_id=to, device_id_type=MESH)

    own_rows = pl.ds(pl.multiple_of(x * TEXT, 8), TEXT)
    in_img = pltpu.make_async_copy(img_hbm, img, in_s.at[0])
    in_txt = pltpu.make_async_copy(txt_hbm.at[own_rows, :], txt, in_s.at[1])
    in_txt.start()
    in_img.start()
    barrier = pltpu.get_barrier_semaphore()
    partners = [at_x(d) for d in range(1, NX)] + [at_y(d) for d in range(1, NY)]
    partners += [at_z(z + d) for d in range(1, NZ)] + [other]
    for to in partners:
        pl.semaphore_signal(barrier, inc=1, device_id=to, device_id_type=MESH)

    def trow(dy):
        return pl.ds(SLOT[dy] * TEXT, TEXT)

    def cols(h):
        return pl.ds(h * HALF, HALF)

    in_txt.wait()
    y_unit, inv_y = unit_rows(txt[...])
    yo[...] = y_unit

    @pl.when(own)
    def _():
        ys[trow(0), :] = y_unit

    in_img.wait()
    for b in range(2):
        rows = pl.ds(b * (BLOCK // 2), BLOCK // 2)
        xo[rows, :] = unit_rows(img[rows, :])[0]

    pl.semaphore_wait(barrier, len(partners))

    def ext(h, dy):
        i = dy if h == 0 else NY
        return rcopy(ys.at[trow(dy), cols(h)], ys.at[trow(dy), cols(h)], e_ss.at[i], e_rs.at[i], at_z(zq))

    def steps(h, right):
        return NY // 2 if right == (h == 0) else NY // 2 - 1

    def ag(h, right, s):
        if right:
            src, dst, to = (NY - (s - 1)) % NY, NY - s, at_y(1)
        else:
            src, dst, to = s - 1, s, at_y(NY - 1)
        i = h * 8 + (0 if right else 4) + s - 1
        return rcopy(ys.at[trow(src), cols(h)], ys.at[trow(dst), cols(h)], ag_ss.at[i], ag_rs.at[i], to)

    @pl.when(own)
    def _():
        ext(1, 0).start()
        for h in range(2):
            for right in (True, False):
                ag(h, right, 1).start()
        ext(0, 0).start()

    QUART = BLOCK // 4
    hx = lax.rem(x, 2)

    def quarter(half, q):
        return pl.ds(pl.multiple_of(half * (BLOCK // 2) + q * QUART, 8), QUART)

    def img_z(q):
        return rcopy(xo.at[quarter(hx, q), :], xs.at[1, quarter(hx, q), :], iz_ss.at[q], iz_rs.at[q], at_z(zp))

    def img_x(q):
        rows = quarter(hx, q)
        to = at_x(1) if q == 0 else at_x(NX - 1)
        return rcopy(xs.at[1, rows, :], xs.at[1, rows, :], ix_ss.at[q], ix_rs.at[q], to)

    def img_core(i):
        if i == 0:
            return rcopy(xo, xs.at[0], ic_ss.at[0], ic_rs.at[0], other)
        rows = quarter(hx, i - 1) if i < 3 else quarter(1 - hx, i - 3)
        return rcopy(xs.at[1, rows, :], xs.at[2, rows, :], ic_ss.at[i], ic_rs.at[i], other)

    for q in range(2):
        img_z(q).start()
    img_core(0).start()

    def put_image(j, block):
        for b in range(2):
            rows = slice(b * (BLOCK // 2), (b + 1) * (BLOCK // 2))
            hi, lo = split_bf16(block[rows, :])
            to = slice(j * BLOCK + b * (BLOCK // 2), j * BLOCK + (b + 1) * (BLOCK // 2))
            xb_hi[to, :] = hi
            xb_lo[to, :] = lo

    def put_text(c):
        rows = slice(c * 2 * TEXT, (c + 1) * 2 * TEXT)
        hi, lo = split_bf16(ys[rows, :])
        yb_hi[rows, :] = hi
        yb_lo[rows, :] = lo

    put_image(0, xo)

    @pl.when(guest)
    def _():
        ext(1, 0).wait_recv()
        for right in (True, False):
            ag(1, right, 1).start()

    scale = jnp.exp(jnp.full((1, 2 * BLOCK), lt_ref[0], F32))
    offset = bias_ref[0]
    lacc[...] = jnp.zeros_like(lacc)

    def pairs(t, half):
        rows = slice(t * TT, (t + 1) * TT)
        at = slice(half * 2 * BLOCK, (half + 1) * 2 * BLOCK)
        prod = dot3(yb_hi[rows, :], yb_lo[rows, :], xb_hi[at, :], xb_lo[at, :], 1, 1)
        logits = scale * prod + offset
        u = jnp.exp(-jnp.abs(logits))
        w = 1.0 + u
        r = 1.0 / w
        sp = jnp.maximum(logits, 0.0) + (jnp.log(w) + (u - (w - 1.0)) * r)
        sig = jnp.where(logits >= 0.0, r, u * r)
        lacc[...] += jnp.sum(sp.reshape(TT // 8, 8, 2 * BLOCK), axis=0)
        hi, lo = split_bf16(sig)
        d_hi[rows, at] = hi
        d_lo[rows, at] = lo

    def text_sums(t):
        rows = slice(t * TT, (t + 1) * TT)
        gy[rows, :] = dot3(d_hi[rows, :], d_lo[rows, :], xb_hi[...], xb_lo[...], 1, 0)

    def ag_step(s):
        @pl.when(own)
        def _():
            for right in (True, False):
                if s <= steps(0, right):
                    ag(0, right, s).wait_recv()
                    if s < steps(0, right):
                        ag(0, right, s + 1).start()
                    ext(0, NY - s if right else s).start()

        for right in (True, False):
            if s <= steps(1, right):
                ag(1, right, s).wait_recv()
                if s < steps(1, right):
                    ag(1, right, s + 1).start()

    def ext_done(*units):
        @pl.when(guest)
        def _():
            for dy in units:
                ext(0, dy).wait_recv()

    ag_step(1)
    img_z(0).wait_recv()
    img_x(0).start()
    img_core(1).start()
    img_core(0).wait_recv()
    put_image(1, xs.at[0])
    ag_step(2)
    img_z(1).wait_recv()
    img_x(1).start()
    img_core(2).start()
    ext_done(1, 7)
    put_text(0)
    img_x(0).wait_recv()
    img_core(3).start()
    ag_step(3)
    ext_done(2, 6)
    put_text(1)
    pairs(0, 0)
    img_x(1).wait_recv()
    img_core(4).start()
    ag_step(4)
    put_image(2, xs.at[1])
    ext_done(3, 5)
    put_text(2)
    for i in range(1, 5):
        img_core(i).wait_recv()
    put_image(3, xs.at[2])
    pairs(0, 1)
    ext_done(0, 4)
    put_text(3)
    pairs(1, 0)
    pairs(1, 1)
    text_sums(1)

    def rs_unit(h, right, s):
        dist = steps(h, right) - s + 1
        return dist if right or dist == 0 else NY - dist

    def rs(h, right, s):
        i = h * 8 + (0 if right else 4) + s - 1
        to = at_y(1 if right else NY - 1)
        return rcopy(gy.at[trow(rs_unit(h, right, s)), cols(h)], rs_in.at[i], rs_ss.at[i], rs_rs.at[i], to)

    def add(dy, h, value):
        at = slice(SLOT[dy] * TEXT, (SLOT[dy] + 1) * TEXT), slice(h * HALF, (h + 1) * HALF)
        gy[at] = gy[at] + value

    def gext(dy):
        return rcopy(gy.at[trow(dy), cols(0)], ge_in.at[dy], ge_ss.at[dy], ge_rs.at[dy], at_z(zq))

    def gfin():
        return rcopy(gy.at[trow(0), cols(1)], gf_in, ge_ss.at[NY], ge_rs.at[NY], at_z(zq))

    def gext_add(dy):
        gext(dy).wait_recv()
        add(dy, 0, ge_in[dy])

    def rs_start(h, s):
        for right in (True, False):
            if s <= steps(h, right):
                rs(h, right, s).start()

    def rs_take(h, s):
        for right in (True, False):
            if s <= steps(h, right):
                rs(h, right, s).wait_recv()
                i = h * 8 + (0 if right else 4) + s - 1
                add(rs_unit(h, right, s + 1), h, rs_in[i])

    @pl.when(guest)
    def _():
        for dy in (4, 3, 5, 0):
            gext(dy).start()

    rs_start(1, 1)
    text_sums(0)

    @pl.when(guest)
    def _():
        for dy in (2, 6, 1, 7):
            gext(dy).start()

    @pl.when(own)
    def _():
        for dy in (4, 5):
            gext_add(dy)
        rs_start(0, 1)

    def gcopy(c):
        return rcopy(gxs.at[c, 1], gc_in.at[c], gc_ss.at[c], gc_rs.at[c], other)

    def image_sums(c):
        at = slice(c * CC, (c + 1) * CC)
        for b in range(2):
            rows = slice(b * 2 * BLOCK, (b + 1) * 2 * BLOCK)
            g = dot3(d_hi[:, rows], d_lo[:, rows], yb_hi[:, at], yb_lo[:, at], 0, 0)
            gxs[c, 0, b] = g[0:BLOCK, :]
            gxs[c, 1, b] = g[BLOCK : 2 * BLOCK, :]
        gcopy(c).start()

    def xrows(d):
        return pl.ds(pl.multiple_of(lax.rem(x + d, NX) * TEXT, 8), TEXT)

    def xa(c, right):
        part = pl.ds(0 if right else CC // 2, CC // 2)
        i = c * 2 + (0 if right else 1)
        src = gxs.at[c, 0, :, xrows(2), part]
        return rcopy(src, xa_in.at[i], xa_ss.at[i], xa_rs.at[i], at_x(1 if right else NX - 1))

    def xf(c, right):
        d = 1 if right else NX - 1
        i = c * 2 + (0 if right else 1)
        return rcopy(gxs.at[c, 0, :, xrows(d), :], xf_in.at[i], xf_ss.at[i], xf_rs.at[i], at_x(d))

    def core_done(c):
        gcopy(c).wait()
        for b in range(2):
            gxs[c, 0, b] = gxs[c, 0, b] + gc_in[c, b]
        for right in (True, False):
            xa(c, right).start()

    def xa_done(c):
        for right in (True, False):
            xa(c, right).wait()
            d = 1 if right else NX - 1
            part = pl.ds(0 if right else CC // 2, CC // 2)
            i = c * 2 + (0 if right else 1)
            for b in range(2):
                gxs[c, 0, b, xrows(d), part] = gxs[c, 0, b, xrows(d), part] + xa_in[i, b]
            xf(c, right).start()

    def q(c, i):
        b, h = (0, 1 - zh) if i == 0 else (1, zh if i == 1 else 1 - zh)
        to = at_z(z + NL) if i == 0 else at_z(zp if i == 1 else zp + NL)
        j = c * 3 + i
        return rcopy(zs.at[c, b, h], zr.at[c, i], q_ss.at[j], q_rs.at[j], to)

    def xf_done(c):
        for right in (True, False):
            xf(c, right).wait()
        for b in range(2):
            v = gxs[c, 0, b, xrows(0), :] + xf_in[c * 2, b] + xf_in[c * 2 + 1, b]
            zs[c, b, 0] = v[0:SHARE, :]
            zs[c, b, 1] = v[SHARE:TEXT, :]
        for i in range(3):
            q(c, i).start()

    image_sums(0)
    image_sums(1)
    image_sums(2)
    core_done(0)

    x_both = xo[xrows(0), :]
    x_own = jnp.where(zh == 0, x_both[0:SHARE, :], x_both[SHARE:TEXT, :])
    y_both = yo[...]
    y_own = jnp.where(zh == 0, y_both[0:SHARE, :], y_both[SHARE:TEXT, :])
    iy_own = jnp.where(zh == 0, inv_y[0:SHARE, :], inv_y[SHARE:TEXT, :])
    scale1 = scale[:, 0:1]
    same = jnp.sum(jnp.sum(x_own * y_own, axis=-1, keepdims=True) * scale1 + offset)
    lc[k] = jnp.full((8, 128), jnp.sum(lacc[...]) - same, F32)

    def lsend(buf, me, ss, rs, to, n):
        copies = [rcopy(buf.at[me], buf.at[me], ss.at[d - 1], rs.at[d - 1], to(d)) for d in range(1, n)]
        for c in copies:
            c.start()
        return copies

    def lsum(buf, copies, n):
        for c in copies:
            c.wait()
        out = buf[0]
        for i in range(1, n):
            out = out + buf[i]
        return out

    def rs_step(s):
        rs_take(1, s)
        rs_start(1, s + 1)

        @pl.when(own)
        def _():
            for dy in ((3, 6), (2, 7), (1,), (0,))[s - 1]:
                gext_add(dy)
            rs_take(0, s)
            rs_start(0, s + 1)

    lcopies = lsend(lc, k, lc_ss, lc_rs, lambda d: other, 2)
    core_done(1)
    rs_step(1)
    core_done(2)
    lx[x] = lsum(lc, lcopies, 2)
    lcopies = lsend(lx, x, lx_ss, lx_rs, at_x, NX)
    xa_done(0)
    rs_step(2)
    xa_done(1)
    xa_done(2)
    ly[y] = lsum(lx, lcopies, NX)
    lcopies = lsend(ly, y, ly_ss, ly_rs, at_y, NY)
    xf_done(0)
    rs_step(3)
    lz[z] = lsum(ly, lcopies, NY)
    lcopies = lsend(lz, z, lz_ss, lz_rs, lambda d: at_z(z + d), NZ)
    xf_done(1)
    rs_step(4)

    @pl.when(guest)
    def _():
        gfin().start()

    hcopy = rcopy(gz.at[1 - zh], gz_in, h_ss, h_rs, at_z(z + NL))

    @pl.when(own)
    def _():
        gfin().wait_recv()
        add(0, 1, gf_in[...])
        gz[0] = gy[SLOT[0] * TEXT : SLOT[0] * TEXT + SHARE, :]
        gz[1] = gy[SLOT[0] * TEXT + SHARE : (SLOT[0] + 1) * TEXT, :]
        hcopy.start()

    xf_done(2)
    loss = lsum(lz, lcopies, NZ) * (1.0 / (float(N) * float(N)))
    loss_o[0] = loss[0, 0]

    for c in range(NC):
        for i in range(3):
            q(c, i).wait()
        gx[:, c * CC : (c + 1) * CC] = zs[c, 0, zh] + zr[c, 0] + zr[c, 1] + zr[c, 2]
    raw = img[xrows(0), :]
    inv_x = unit_rows(jnp.where(zh == 0, raw[0:SHARE, :], raw[SHARE:TEXT, :]))[1]
    g = scale1 * (gx[...] - y_own)
    gi_o[...] = inv_x * (g - x_own * jnp.sum(x_own * g, axis=-1, keepdims=True))

    @pl.when(own)
    def _():
        gt[...] = gz[zh]

    @pl.when(guest)
    def _():
        hcopy.wait_recv()
        gt[...] = gz_in[...]

    g = scale1 * (gt[...] - x_own)
    gt_o[...] = iy_own * (g - y_own * jnp.sum(y_own * g, axis=-1, keepdims=True))

    for i in range(2):
        img_z(i).wait_send()
        img_x(i).wait_send()
    for i in range(5):
        img_core(i).wait_send()
    for right in (True, False):
        for s in range(1, steps(1, right) + 1):
            ag(1, right, s).wait_send()
            rs(1, right, s).wait_send()

    @pl.when(own)
    def _():
        ext(1, 0).wait_send()
        for dy in range(NY):
            ext(0, dy).wait_send()
        for right in (True, False):
            for s in range(1, steps(0, right) + 1):
                ag(0, right, s).wait_send()
                rs(0, right, s).wait_send()
        hcopy.wait_send()

    @pl.when(guest)
    def _():
        for dy in range(NY):
            gext(dy).wait_send()
        gfin().wait_send()


def local(image, text, log_temp, bias):
    vmem = pl.BlockSpec(memory_space=pltpu.VMEM)
    smem = pl.BlockSpec(memory_space=pltpu.SMEM)
    hbm = pl.BlockSpec(memory_space=pl.ANY)
    dma = pltpu.SemaphoreType.DMA
    scratch = [
        pltpu.VMEM((BLOCK, D), F32),
        pltpu.VMEM((TEXT, D), F32),
        pltpu.VMEM((BLOCK, D), F32),
        pltpu.VMEM((TEXT, D), F32),
        pltpu.VMEM((3, BLOCK, D), F32),
        pltpu.VMEM((T, D), F32),
        pltpu.VMEM((S, D), BF16),
        pltpu.VMEM((S, D), BF16),
        pltpu.VMEM((T, D), BF16),
        pltpu.VMEM((T, D), BF16),
        pltpu.VMEM((T, S), BF16),
        pltpu.VMEM((T, S), BF16),
        pltpu.VMEM((T, D), F32),
        pltpu.VMEM((NY, TEXT, HALF), F32),
        pltpu.VMEM((TEXT, HALF), F32),
        pltpu.VMEM((16, TEXT, HALF), F32),
        pltpu.VMEM((2, SHARE, D), F32),
        pltpu.VMEM((SHARE, D), F32),
        pltpu.VMEM((SHARE, D), F32),
        pltpu.VMEM((NC, 2, 2, BLOCK, CC), F32),
        pltpu.VMEM((NC, 2, BLOCK, CC), F32),
        pltpu.VMEM((2 * NC, 2, TEXT, CC // 2), F32),
        pltpu.VMEM((2 * NC, 2, TEXT, CC), F32),
        pltpu.VMEM((NC, 2, 2, SHARE, CC), F32),
        pltpu.VMEM((NC, 3, SHARE, CC), F32),
        pltpu.VMEM((SHARE, D), F32),
        pltpu.VMEM((8, 2 * BLOCK), F32),
        pltpu.VMEM((2, 8, 128), F32),
        pltpu.VMEM((NX, 8, 128), F32),
        pltpu.VMEM((NY, 8, 128), F32),
        pltpu.VMEM((NZ, 8, 128), F32),
        dma((2,)),
    ]
    for n in (NY + 1, 16, 5, 2, 2, NY + 1, 16, NC, 2 * NC, 2 * NC, 3 * NC):
        scratch += [dma((n,)), dma((n,))]
    scratch += [dma, dma]
    for n in (1, NX - 1, NY - 1, NZ - 1):
        scratch += [dma((n,)), dma((n,))]
    loss, gi, gt = pl.pallas_call(
        kernel,
        out_shape=(
            jax.ShapeDtypeStruct((1,), F32),
            jax.ShapeDtypeStruct((SHARE, D), F32),
            jax.ShapeDtypeStruct((SHARE, D), F32),
        ),
        in_specs=[hbm, hbm, smem, smem],
        out_specs=(smem, vmem, vmem),
        scratch_shapes=scratch,
        compiler_params=pltpu.CompilerParams(
            collective_id=0, has_side_effects=True, vmem_limit_bytes=56 << 20
        ),
    )(image, text, log_temp, bias)
    return loss[0], gi, gt


def solution(mesh):
    in_specs = (P("dp", None), P("dp", None), P(), P())
    out_specs = (P(), P(("dp", "split"), None), P(("dp", "split"), None))
    return jax.shard_map(local, mesh=mesh, in_specs=in_specs, out_specs=out_specs, check_vma=False)
```

```python
import jax
import jax.numpy as jnp
from jax import lax
from jax.experimental import pallas as pl
from jax.experimental.pallas import tpu as pltpu
from jax.sharding import PartitionSpec as P

EPS = 1e-06
MESH = pl.DeviceIdType.MESH
D = 768
NX, NY, NZ, NL = 4, 8, 8, 4
N = 14336
SHARE = 28
BLOCK = 224
TEXT = 56
GROUP = NX * SHARE
S = 2 * NL * GROUP
ORDER = (0, 1, 3, 2)
T = NY * TEXT
HALF = D // 2
NC = 3
CC = D // NC
LANES = 6
LW = D // LANES
TT = T // 2
F32 = jnp.float32
BF16 = jnp.bfloat16
SLOT = {1: 0, 7: 1, 2: 2, 6: 3, 3: 4, 5: 5, 0: 6, 4: 7}


def split_bf16(v):
    hi = v.astype(BF16)
    return hi, (v - hi.astype(F32)).astype(BF16)


def dot3(ah, al, bh, bl, ca, cb):
    def one(a, b):
        return lax.dot_general(a, b, (((ca,), (cb,)), ((), ())), preferred_element_type=F32)

    return one(ah, bh) + one(al, bh) + one(ah, bl)


def unit_rows(v):
    inv = lax.rsqrt(jnp.sum(v * v, axis=-1, keepdims=True) + EPS)
    return v * inv, inv


def kernel(
    img_hbm, txt_hbm, lt_ref, bias_ref,
    loss_o, gi_o, gt_o,
    img, txt, xh, invx, xo, yo, xs, xc, ys, xb_hi, xb_lo, yb_hi, yb_lo, d_hi, d_lo,
    gy, rs_in, gz, gz_in, gxs, gc_in, xa_in, xf_in, zs, zr, gx, lacc, lc, lx, ly, lz,
    in_s, ag_ss, ag_rs, ic_ss, ic_rs, iz_ss, iz_rs, ix_ss, ix_rs,
    rs_ss, rs_rs, gc_ss, gc_rs, xa_ss, xa_rs, xf_ss, xf_rs, q_ss, q_rs, h_ss, h_rs,
    lc_ss, lc_rs, lx_ss, lx_rs, ly_ss, ly_rs, lz_ss, lz_rs,
):
    dp = lax.axis_index("dp")
    split = lax.axis_index("split")
    k = lax.rem(dp, 2)
    y = lax.rem(lax.div(dp, 2), NY)
    zl = lax.div(dp, 2 * NY)
    x = lax.div(split, 2)
    zh = lax.rem(split, 2)
    z = zh * NL + zl
    def dev(x_, y_, z_, k_):
        return (lax.rem(z_, NL) * (2 * NY) + y_ * 2 + k_, x_ * 2 + lax.div(z_, NL))

    def at_x(d):
        return dev(lax.rem(x + d, NX), y, z, k)

    def at_y(d):
        return dev(x, lax.rem(y + d, NY), z, k)

    def at_z(z_):
        return dev(x, y, lax.rem(z_, NZ), k)

    def at_line(r):
        return dev(x, y, zh * NL + lax.rem(zl + r, NL), k)

    other = dev(x, y, z, 1 - k)

    def rcopy(src, dst, ss, rs, to):
        return pltpu.make_async_remote_copy(src, dst, ss, rs, device_id=to, device_id_type=MESH)

    own_rows = pl.ds(pl.multiple_of(x * TEXT, 8), TEXT)
    in_img = pltpu.make_async_copy(img_hbm, img, in_s.at[0])
    in_txt = pltpu.make_async_copy(txt_hbm.at[own_rows, :], txt, in_s.at[1])
    in_txt.start()
    in_img.start()
    barrier = pltpu.get_barrier_semaphore()
    partners = [at_x(d) for d in range(1, NX)] + [at_y(d) for d in range(1, NY)]
    partners += [at_z(z + d) for d in range(1, NZ)] + [other]
    for to in partners:
        pl.semaphore_signal(barrier, inc=1, device_id=to, device_id_type=MESH)

    def trow(dy):
        return pl.ds(SLOT[dy] * TEXT, TEXT)

    in_txt.wait()
    y_unit, inv_y = unit_rows(txt[...])
    yo[...] = y_unit
    ys[trow(0), :] = y_unit
    in_img.wait()
    for i in range(2 * NX):
        unit, inv = unit_rows(img[i * SHARE : (i + 1) * SHARE, :])
        xh[i % 2, i // 2] = unit
        invx[i % 2, i // 2] = jnp.broadcast_to(inv, (SHARE, 128))
        xo[i % 2, i // 2 * SHARE : (i // 2 + 1) * SHARE, :] = unit

    pl.semaphore_wait(barrier, len(partners))

    def lane_cols(n):
        return pl.ds(n * LW, LW)

    def steps(n, right):
        return NY // 2 if right == (n % 2 == 0) else NY // 2 - 1

    def ag(n, right, s):
        if right:
            src, dst, to = (NY - (s - 1)) % NY, NY - s, at_y(1)
        else:
            src, dst, to = s - 1, s, at_y(NY - 1)
        i = n * 8 + (0 if right else 4) + s - 1
        return rcopy(ys.at[trow(src), lane_cols(n)], ys.at[trow(dst), lane_cols(n)], ag_ss.at[i], ag_rs.at[i], to)

    for n in range(LANES):
        for right in (True, False):
            ag(n, right, 1).start()

    hx = lax.rem(x, 2)

    def half(h):
        return pl.ds(pl.multiple_of(h * HALF, 128), HALF)

    def img_z(r):
        z_ = z + {1: NZ - 1, 3: 1}[r] if r != 2 else z + 2 + NL * k
        there = lax.div(lax.rem(z_, NZ), NL)
        return rcopy(xo.at[there, :, half(hx)], xs.at[r - 1, :, half(hx)], iz_ss.at[r - 1], iz_rs.at[r - 1], at_z(z_))

    def img_x(r, right):
        i = (r - 1) * 2 + (0 if right else 1)
        ref = xs.at[r - 1, pl.ds(0 if right else GROUP // 2, GROUP // 2), half(hx)]
        return rcopy(ref, ref, ix_ss.at[i], ix_rs.at[i], at_x(1 if right else NX - 1))

    def core_z(r):
        return rcopy(xs.at[r - 1, :, half(hx)], xc.at[r, :, half(hx)], ic_ss.at[r], ic_rs.at[r], other)

    def core_x(r, right):
        i = NL + (r - 1) * 2 + (0 if right else 1)
        rows = pl.ds(0 if right else GROUP // 2, GROUP // 2)
        src = xs.at[r - 1, rows, half(1 - hx)]
        return rcopy(src, xc.at[r, rows, half(1 - hx)], ic_ss.at[i], ic_rs.at[i], other)

    core_own = rcopy(xo.at[zh], xc.at[0], ic_ss.at[0], ic_rs.at[0], other)
    for r in (1, 3, 2):
        img_z(r).start()
    core_own.start()

    def from_z(r):
        img_z(r).wait_recv()
        for right in (True, False):
            img_x(r, right).start()
        core_z(r).start()

    def from_x(r):
        for right in (True, False):
            img_x(r, right).wait_recv()
            core_x(r, right).start()

    def from_core(r):
        core_z(r).wait_recv()
        for right in (True, False):
            core_x(r, right).wait_recv()

    def put_image(r, block, kk):
        g = ORDER.index(r) * 2 + kk
        rows = slice(g * GROUP, (g + 1) * GROUP)
        hi, lo = split_bf16(block)
        xb_hi[rows, :] = hi
        xb_lo[rows, :] = lo

    def put_text(c):
        rows = slice(c * 2 * TEXT, (c + 1) * 2 * TEXT)
        hi, lo = split_bf16(ys[rows, :])
        yb_hi[rows, :] = hi
        yb_lo[rows, :] = lo

    put_image(0, xo[zh], 0)

    scale = jnp.exp(jnp.full((1, S // 2), lt_ref[0], F32))
    offset = bias_ref[0]
    lacc[...] = jnp.zeros_like(lacc)

    def pairs(t, half):
        rows = slice(t * TT, (t + 1) * TT)
        at = slice(half * S // 2, (half + 1) * S // 2)
        prod = dot3(yb_hi[rows, :], yb_lo[rows, :], xb_hi[at, :], xb_lo[at, :], 1, 1)
        logits = scale * prod + offset
        u = jnp.exp(-jnp.abs(logits))
        w = 1.0 + u
        r = 1.0 / w
        sp = jnp.maximum(logits, 0.0) + (jnp.log(w) + (u - (w - 1.0)) * r)
        sig = jnp.where(logits >= 0.0, r, u * r)
        lacc[...] += jnp.sum(sp.reshape(TT // 8, 8, S // 2), axis=0)
        hi, lo = split_bf16(sig)
        d_hi[rows, at] = hi
        d_lo[rows, at] = lo

    def text_sums(t):
        rows = slice(t * TT, (t + 1) * TT)
        gy[rows, :] = dot3(d_hi[rows, :], d_lo[rows, :], xb_hi[...], xb_lo[...], 1, 0)

    def ag_take(s):
        for n in range(LANES):
            for right in (True, False):
                if s <= steps(n, right):
                    ag(n, right, s).wait_recv()
                    if s < steps(n, right):
                        ag(n, right, s + 1).start()

    ag_take(1)
    core_own.wait_recv()
    put_image(0, xc[0], 1)
    put_text(0)
    from_z(1)
    from_z(3)
    ag_take(2)
    put_text(1)
    ag_take(3)
    put_text(2)
    from_z(2)
    from_x(1)
    put_image(1, xs[0], 0)
    from_x(3)
    put_image(3, xs[2], 0)
    ag_take(4)
    put_text(3)
    from_core(1)
    put_image(1, xc[1], 1)
    pairs(1, 0)
    from_x(2)
    put_image(2, xs[1], 0)
    pairs(0, 0)
    from_core(3)
    put_image(3, xc[3], 1)
    from_core(2)
    put_image(2, xc[2], 1)
    pairs(1, 1)
    pairs(0, 1)

    x_own = xh[zh, x]
    y_both = yo[...]
    y_own = jnp.where(zh == 0, y_both[0:SHARE, :], y_both[SHARE:TEXT, :])
    iy_own = jnp.where(zh == 0, inv_y[0:SHARE, :], inv_y[SHARE:TEXT, :])
    scale1 = scale[:, 0:1]
    same = jnp.sum(jnp.sum(x_own * y_own, axis=-1, keepdims=True) * scale1 + offset)
    lc[k] = jnp.full((8, 128), jnp.sum(lacc[...]) - same, F32)

    def lsend(buf, me, ss, rs, to, n):
        copies = [rcopy(buf.at[me], buf.at[me], ss.at[d - 1], rs.at[d - 1], to(d)) for d in range(1, n)]
        for c in copies:
            c.start()
        return copies

    def lsum(buf, copies, n):
        for c in copies:
            c.wait()
        out = buf[0]
        for i in range(1, n):
            out = out + buf[i]
        return out

    lcopies = lsend(lc, k, lc_ss, lc_rs, lambda d: other, 2)

    def rs_unit(n, right, s):
        dist = steps(n, right) - s + 1
        return dist if right or dist == 0 else NY - dist

    def rs(n, right, s):
        i = n * 8 + (0 if right else 4) + s - 1
        to = at_y(1 if right else NY - 1)
        src = gy.at[trow(rs_unit(n, right, s)), lane_cols(n)]
        return rcopy(src, rs_in.at[i], rs_ss.at[i], rs_rs.at[i], to)

    def rs_start():
        for n in range(LANES):
            for right in (True, False):
                rs(n, right, 1).start()

    def rs_take(s):
        for n in range(LANES):
            for right in (True, False):
                if s <= steps(n, right):
                    rs(n, right, s).wait_recv()
                    i = n * 8 + (0 if right else 4) + s - 1
                    unit = rs_unit(n, right, s + 1)
                    at = slice(SLOT[unit] * TEXT, (SLOT[unit] + 1) * TEXT), slice(n * LW, (n + 1) * LW)
                    gy[at] = gy[at] + rs_in[i]
                    if s < steps(n, right):
                        rs(n, right, s + 1).start()

    def gcopy(c):
        return rcopy(gxs.at[c, 1], gc_in.at[c], gc_ss.at[c], gc_rs.at[c], other)

    def image_sums(c):
        at = slice(c * CC, (c + 1) * CC)
        for b in range(2):
            rows = slice(b * S // 2, (b + 1) * S // 2)
            g = dot3(d_hi[:, rows], d_lo[:, rows], yb_hi[:, at], yb_lo[:, at], 0, 0)
            for i in range(NL):
                r = ORDER[b * 2 + i // 2]
                for j in range(NX):
                    gxs[c, i % 2, j, r] = g[i * GROUP + j * SHARE : i * GROUP + (j + 1) * SHARE, :]
        gcopy(c).start()

    def ahead(d):
        return lax.rem(x + d, NX)

    def xa(c, right):
        b = 0 if right else 1
        i = c * 2 + b
        src = gxs.at[c, 0, ahead(2), pl.ds(b * 2, 2)]
        return rcopy(src, xa_in.at[i], xa_ss.at[i], xa_rs.at[i], at_x(1 if right else NX - 1))

    def xf(c, right):
        d = 1 if right else NX - 1
        i = c * 2 + (0 if right else 1)
        return rcopy(gxs.at[c, 0, ahead(d)], xf_in.at[i], xf_ss.at[i], xf_rs.at[i], at_x(d))

    def core_done(c):
        gcopy(c).wait()
        for j in range(NX):
            gxs[c, 0, j] = gxs[c, 0, j] + gc_in[c, j]
        for right in (True, False):
            xa(c, right).start()

    def xa_done(c):
        for right in (True, False):
            xa(c, right).wait()
            d = 1 if right else NX - 1
            b = 0 if right else 1
            for i in range(2):
                r = b * 2 + i
                gxs[c, 0, ahead(d), r] = gxs[c, 0, ahead(d), r] + xa_in[c * 2 + b, i]
            xf(c, right).start()

    def q(c, r):
        i = c * 3 + r - 1
        return rcopy(zs.at[c, r], zr.at[c, r - 1], q_ss.at[i], q_rs.at[i], at_line(r))

    def xf_done(c):
        for right in (True, False):
            xf(c, right).wait()
        zs[c] = gxs[c, 0, x] + xf_in[c * 2] + xf_in[c * 2 + 1]
        for r in (2, 1, 3):
            q(c, r).start()

    image_sums(0)
    text_sums(1)
    rs_start()
    core_done(0)
    text_sums(0)
    image_sums(1)
    lx[x] = lsum(lc, lcopies, 2)
    lcopies = lsend(lx, x, lx_ss, lx_rs, at_x, NX)
    core_done(1)
    rs_take(1)
    image_sums(2)
    xa_done(0)
    core_done(2)
    xa_done(1)
    ly[y] = lsum(lx, lcopies, NX)
    lcopies = lsend(ly, y, ly_ss, ly_rs, at_y, NY)
    rs_take(2)
    xf_done(0)
    xa_done(2)
    rs_take(3)
    xf_done(1)
    lz[z] = lsum(ly, lcopies, NY)
    lcopies = lsend(lz, z, lz_ss, lz_rs, lambda d: at_z(z + d), NZ)
    rs_take(4)
    gz[0] = gy[SLOT[0] * TEXT : SLOT[0] * TEXT + SHARE, :]
    gz[1] = gy[SLOT[0] * TEXT + SHARE : (SLOT[0] + 1) * TEXT, :]
    hcopy = rcopy(gz.at[1 - zh], gz_in, h_ss, h_rs, at_z(z + NL))
    hcopy.start()
    xf_done(2)
    loss = lsum(lz, lcopies, NZ) * (1.0 / (float(N) * float(N)))
    loss_o[0] = loss[0, 0]

    for c in range(NC):
        for r in range(1, NL):
            q(c, r).wait()
        gx[:, c * CC : (c + 1) * CC] = zs[c, 0] + zr[c, 0] + zr[c, 1] + zr[c, 2]
    inv_x = invx[zh, x][:, 0:1]
    g = scale1 * (gx[...] - y_own)
    gi_o[...] = inv_x * (g - x_own * jnp.sum(x_own * g, axis=-1, keepdims=True))

    hcopy.wait()
    g = scale1 * (gz[zh] + gz_in[...] - x_own)
    gt_o[...] = iy_own * (g - y_own * jnp.sum(y_own * g, axis=-1, keepdims=True))

    core_own.wait_send()
    for r in range(1, NL):
        img_z(r).wait_send()
        core_z(r).wait_send()
        for right in (True, False):
            img_x(r, right).wait_send()
            core_x(r, right).wait_send()
    for n in range(LANES):
        for right in (True, False):
            for s in range(1, steps(n, right) + 1):
                ag(n, right, s).wait_send()
                rs(n, right, s).wait_send()


def local(image, text, log_temp, bias):
    vmem = pl.BlockSpec(memory_space=pltpu.VMEM)
    smem = pl.BlockSpec(memory_space=pltpu.SMEM)
    hbm = pl.BlockSpec(memory_space=pl.ANY)
    dma = pltpu.SemaphoreType.DMA
    scratch = [
        pltpu.VMEM((BLOCK, D), F32),
        pltpu.VMEM((TEXT, D), F32),
        pltpu.VMEM((2, NX, SHARE, D), F32),
        pltpu.VMEM((2, NX, SHARE, 128), F32),
        pltpu.VMEM((2, GROUP, D), F32),
        pltpu.VMEM((TEXT, D), F32),
        pltpu.VMEM((NL - 1, GROUP, D), F32),
        pltpu.VMEM((NL, GROUP, D), F32),
        pltpu.VMEM((T, D), F32),
        pltpu.VMEM((S, D), BF16),
        pltpu.VMEM((S, D), BF16),
        pltpu.VMEM((T, D), BF16),
        pltpu.VMEM((T, D), BF16),
        pltpu.VMEM((T, S), BF16),
        pltpu.VMEM((T, S), BF16),
        pltpu.VMEM((T, D), F32),
        pltpu.VMEM((8 * LANES, TEXT, LW), F32),
        pltpu.VMEM((2, SHARE, D), F32),
        pltpu.VMEM((SHARE, D), F32),
        pltpu.VMEM((NC, 2, NX, NL, SHARE, CC), F32),
        pltpu.VMEM((NC, NX, NL, SHARE, CC), F32),
        pltpu.VMEM((2 * NC, 2, SHARE, CC), F32),
        pltpu.VMEM((2 * NC, NL, SHARE, CC), F32),
        pltpu.VMEM((NC, NL, SHARE, CC), F32),
        pltpu.VMEM((NC, NL - 1, SHARE, CC), F32),
        pltpu.VMEM((SHARE, D), F32),
        pltpu.VMEM((8, S // 2), F32),
        pltpu.VMEM((2, 8, 128), F32),
        pltpu.VMEM((NX, 8, 128), F32),
        pltpu.VMEM((NY, 8, 128), F32),
        pltpu.VMEM((NZ, 8, 128), F32),
        dma((2,)),
    ]
    for n in (8 * LANES, 10, 3, 6, 8 * LANES, NC, 2 * NC, 2 * NC, 3 * NC):
        scratch += [dma((n,)), dma((n,))]
    scratch += [dma, dma]
    for n in (1, NX - 1, NY - 1, NZ - 1):
        scratch += [dma((n,)), dma((n,))]
    loss, gi, gt = pl.pallas_call(
        kernel,
        out_shape=(
            jax.ShapeDtypeStruct((1,), F32),
            jax.ShapeDtypeStruct((SHARE, D), F32),
            jax.ShapeDtypeStruct((SHARE, D), F32),
        ),
        in_specs=[hbm, hbm, smem, smem],
        out_specs=(smem, vmem, vmem),
        scratch_shapes=scratch,
        compiler_params=pltpu.CompilerParams(
            collective_id=0, has_side_effects=True, vmem_limit_bytes=56 << 20
        ),
    )(image, text, log_temp, bias)
    return loss[0], gi, gt


def solution(mesh):
    in_specs = (P("dp", None), P("dp", None), P(), P())
    out_specs = (P(), P(("dp", "split"), None), P(("dp", "split"), None))
    return jax.shard_map(local, mesh=mesh, in_specs=in_specs, out_specs=out_specs, check_vma=False)
```

```python
import jax
import jax.numpy as jnp
from jax import lax
from jax.experimental import pallas as pl
from jax.experimental.pallas import tpu as pltpu
from jax.sharding import PartitionSpec as P

EPS = 1e-06
MESH = pl.DeviceIdType.MESH
D = 768
NX, NY, NZ, NL = 4, 8, 8, 4
N = 14336
SHARE = 28
BLOCK = 224
TEXT = 56
GROUP = NX * SHARE
S = 2 * NL * GROUP
ORDER = (0, 1, 3, 2)
T = NY * TEXT
HALF = D // 2
NC = 3
CC = D // NC
LANES = 3
LW = D // LANES
TT = T // 2
F32 = jnp.float32
BF16 = jnp.bfloat16
SLOT = {1: 0, 7: 1, 2: 2, 6: 3, 3: 4, 5: 5, 0: 6, 4: 7}


def split_bf16(v):
    hi = v.astype(BF16)
    return hi, (v - hi.astype(F32)).astype(BF16)


def dot3(ah, al, bh, bl, ca, cb):
    def one(a, b):
        return lax.dot_general(a, b, (((ca,), (cb,)), ((), ())), preferred_element_type=F32)

    return one(ah, bh) + one(al, bh) + one(ah, bl)


def unit_rows(v):
    inv = lax.rsqrt(jnp.sum(v * v, axis=-1, keepdims=True) + EPS)
    return v * inv, inv


def kernel(
    img_hbm, txt_hbm, lt_ref, bias_ref,
    loss_o, gi_o, gt_o,
    img, txt, xo, yo, xs, xc, ys, xb_hi, xb_lo, yb_hi, yb_lo, d_hi, d_lo,
    gy, rs_in, gz, gz_in, gxs, gc_in, xa_in, xf_in, zs, zr, gx, lacc, lc, lx, ly, lz,
    in_s, ag_ss, ag_rs, ic_ss, ic_rs, iz_ss, iz_rs, ix_ss, ix_rs,
    rs_ss, rs_rs, gc_ss, gc_rs, xa_ss, xa_rs, xf_ss, xf_rs, q_ss, q_rs, h_ss, h_rs,
    lc_ss, lc_rs, lx_ss, lx_rs, ly_ss, ly_rs, lz_ss, lz_rs,
):
    dp = lax.axis_index("dp")
    split = lax.axis_index("split")
    k = lax.rem(dp, 2)
    y = lax.rem(lax.div(dp, 2), NY)
    zl = lax.div(dp, 2 * NY)
    x = lax.div(split, 2)
    zh = lax.rem(split, 2)
    z = zh * NL + zl
    def dev(x_, y_, z_, k_):
        return (lax.rem(z_, NL) * (2 * NY) + y_ * 2 + k_, x_ * 2 + lax.div(z_, NL))

    def at_x(d):
        return dev(lax.rem(x + d, NX), y, z, k)

    def at_y(d):
        return dev(x, lax.rem(y + d, NY), z, k)

    def at_z(z_):
        return dev(x, y, lax.rem(z_, NZ), k)

    def at_line(r):
        return dev(x, y, zh * NL + lax.rem(zl + r, NL), k)

    other = dev(x, y, z, 1 - k)

    def rcopy(src, dst, ss, rs, to):
        return pltpu.make_async_remote_copy(src, dst, ss, rs, device_id=to, device_id_type=MESH)

    own_rows = pl.ds(pl.multiple_of(x * TEXT, 8), TEXT)
    in_img = pltpu.make_async_copy(img_hbm, img, in_s.at[0])
    in_txt = pltpu.make_async_copy(txt_hbm.at[own_rows, :], txt, in_s.at[1])
    in_txt.start()
    in_img.start()
    barrier = pltpu.get_barrier_semaphore()
    partners = [at_x(d) for d in range(1, NX)] + [at_y(d) for d in range(1, NY)]
    partners += [at_z(z + d) for d in range(1, NZ)] + [other]
    for to in partners:
        pl.semaphore_signal(barrier, inc=1, device_id=to, device_id_type=MESH)

    def trow(dy):
        return pl.ds(SLOT[dy] * TEXT, TEXT)

    in_txt.wait()
    y_unit, inv_y = unit_rows(txt[...])
    yo[...] = y_unit
    ys[trow(0), :] = y_unit
    pl.semaphore_wait(barrier, len(partners))

    def lane_cols(n):
        return pl.ds(n * LW, LW)

    def steps(n, right):
        return NY // 2 if right == (n % 2 == 0) else NY // 2 - 1

    def ag(n, right, s):
        if right:
            src, dst, to = (NY - (s - 1)) % NY, NY - s, at_y(1)
        else:
            src, dst, to = s - 1, s, at_y(NY - 1)
        i = n * 8 + (0 if right else 4) + s - 1
        return rcopy(ys.at[trow(src), lane_cols(n)], ys.at[trow(dst), lane_cols(n)], ag_ss, ag_rs.at[i], to)

    for n in range(LANES):
        for right in (True, False):
            ag(n, right, 1).start()

    in_img.wait()
    unit = unit_rows(img[...])[0]
    for i in range(2 * NX):
        xo[i % 2, i // 2 * SHARE : (i // 2 + 1) * SHARE, :] = unit[i * SHARE : (i + 1) * SHARE, :]

    hx = lax.rem(x, 2)

    def half(h):
        return pl.ds(pl.multiple_of(h * HALF, 128), HALF)

    def img_z(r):
        z_ = z + {1: NZ - 1, 3: 1}[r] if r != 2 else z + 2 + NL * k
        there = lax.div(lax.rem(z_, NZ), NL)
        return rcopy(xo.at[there, :, half(hx)], xs.at[r - 1, :, half(hx)], iz_ss.at[r - 1], iz_rs.at[r - 1], at_z(z_))

    def img_x(r, right):
        i = (r - 1) * 2 + (0 if right else 1)
        ref = xs.at[r - 1, pl.ds(0 if right else GROUP // 2, GROUP // 2), half(hx)]
        return rcopy(ref, ref, ix_ss.at[i], ix_rs.at[i], at_x(1 if right else NX - 1))

    def core_z(r):
        return rcopy(xs.at[r - 1, :, half(hx)], xc.at[r, :, half(hx)], ic_ss.at[r], ic_rs.at[r], other)

    def core_x(r, right):
        i = NL + (r - 1) * 2 + (0 if right else 1)
        rows = pl.ds(0 if right else GROUP // 2, GROUP // 2)
        src = xs.at[r - 1, rows, half(1 - hx)]
        return rcopy(src, xc.at[r, rows, half(1 - hx)], ic_ss.at[i], ic_rs.at[i], other)

    core_own = rcopy(xo.at[zh], xc.at[0], ic_ss.at[0], ic_rs.at[0], other)
    for r in (1, 3, 2):
        img_z(r).start()
    core_own.start()

    def from_z(r):
        img_z(r).wait()
        for right in (True, False):
            img_x(r, right).start()
        core_z(r).start()

    def from_x(r):
        for right in (True, False):
            img_x(r, right).wait()
            core_x(r, right).start()

    def from_core(r):
        core_z(r).wait()
        for right in (True, False):
            core_x(r, right).wait()

    def put_image(r, block, kk):
        g = ORDER.index(r) * 2 + kk
        rows = slice(g * GROUP, (g + 1) * GROUP)
        hi, lo = split_bf16(block)
        xb_hi[rows, :] = hi
        xb_lo[rows, :] = lo

    def put_text(c):
        rows = slice(c * 2 * TEXT, (c + 1) * 2 * TEXT)
        hi, lo = split_bf16(ys[rows, :])
        yb_hi[rows, :] = hi
        yb_lo[rows, :] = lo

    put_image(0, xo[zh], 0)

    scale = jnp.exp(jnp.full((1, S // 2), lt_ref[0], F32))
    offset = bias_ref[0]
    lacc[...] = jnp.zeros_like(lacc)

    def pairs(t, half):
        rows = slice(t * TT, (t + 1) * TT)
        at = slice(half * S // 2, (half + 1) * S // 2)
        prod = dot3(yb_hi[rows, :], yb_lo[rows, :], xb_hi[at, :], xb_lo[at, :], 1, 1)
        logits = scale * prod + offset
        u = jnp.exp(-jnp.abs(logits))
        w = 1.0 + u
        r = 1.0 / w
        sp = jnp.maximum(logits, 0.0) + (jnp.log(w) + (u - (w - 1.0)) * r)
        sig = jnp.where(logits >= 0.0, r, u * r)
        lacc[...] += jnp.sum(sp.reshape(TT // 8, 8, S // 2), axis=0)
        hi, lo = split_bf16(sig)
        d_hi[rows, at] = hi
        d_lo[rows, at] = lo

    def text_sums(t):
        rows = slice(t * TT, (t + 1) * TT)
        gy[rows, :] = dot3(d_hi[rows, :], d_lo[rows, :], xb_hi[...], xb_lo[...], 1, 0)

    def ag_take(s):
        for n in range(LANES):
            for right in (True, False):
                if s <= steps(n, right):
                    ag(n, right, s).wait_recv()
                    if s < steps(n, right):
                        ag(n, right, s + 1).start()

    ag_take(1)
    core_own.wait()
    put_image(0, xc[0], 1)
    from_z(1)
    from_z(3)
    put_text(0)
    ag_take(2)
    put_text(1)
    from_z(2)
    ag_take(3)
    put_text(2)
    from_x(1)
    from_x(3)
    put_image(1, xs[0], 0)
    put_image(3, xs[2], 0)
    from_core(1)
    put_image(1, xc[1], 1)
    pairs(0, 0)
    from_x(2)
    from_core(3)
    put_image(3, xc[3], 1)
    put_image(2, xs[1], 0)
    from_core(2)
    put_image(2, xc[2], 1)
    pairs(0, 1)
    ag_take(4)
    put_text(3)
    pairs(1, 0)
    pairs(1, 1)

    sent = pl.ds(0, (NY - 1) * TEXT)
    rcopy(ys.at[sent, :], ys.at[sent, :], ag_ss, ag_rs.at[0], other).wait_send()

    raw = img[0:SHARE, :]
    for i in range(1, 2 * NX):
        raw = jnp.where(split == i, img[i * SHARE : (i + 1) * SHARE, :], raw)
    x_own, inv_x = unit_rows(raw)
    y_both = yo[...]
    y_own = jnp.where(zh == 0, y_both[0:SHARE, :], y_both[SHARE:TEXT, :])
    iy_own = jnp.where(zh == 0, inv_y[0:SHARE, :], inv_y[SHARE:TEXT, :])
    scale1 = scale[:, 0:1]
    same = jnp.sum(jnp.sum(x_own * y_own, axis=-1, keepdims=True) * scale1 + offset)
    lc[k] = jnp.full((8, 128), jnp.sum(lacc[...]) - same, F32)

    def lsend(buf, me, ss, rs, to, n):
        copies = [rcopy(buf.at[me], buf.at[me], ss.at[d - 1], rs.at[d - 1], to(d)) for d in range(1, n)]
        for c in copies:
            c.start()
        return copies

    def lsum(buf, copies, n):
        for c in copies:
            c.wait()
        out = buf[0]
        for i in range(1, n):
            out = out + buf[i]
        return out

    lcopies = lsend(lc, k, lc_ss, lc_rs, lambda d: other, 2)

    def rs_unit(n, right, s):
        dist = steps(n, right) - s + 1
        return dist if right or dist == 0 else NY - dist

    def rs(n, right, s):
        i = n * 8 + (0 if right else 4) + s - 1
        to = at_y(1 if right else NY - 1)
        src = gy.at[trow(rs_unit(n, right, s)), lane_cols(n)]
        return rcopy(src, rs_in.at[i], rs_ss, rs_rs.at[i], to)

    def rs_start():
        for n in range(LANES):
            for right in (True, False):
                rs(n, right, 1).start()

    def rs_take(s):
        for n in range(LANES):
            for right in (True, False):
                if s <= steps(n, right):
                    rs(n, right, s).wait_recv()
                    i = n * 8 + (0 if right else 4) + s - 1
                    unit = rs_unit(n, right, s + 1)
                    at = slice(SLOT[unit] * TEXT, (SLOT[unit] + 1) * TEXT), slice(n * LW, (n + 1) * LW)
                    gy[at] = gy[at] + rs_in[i]
                    if s < steps(n, right):
                        rs(n, right, s + 1).start()

    def gcopy(c):
        return rcopy(gxs.at[c, 1], gc_in.at[c], gc_ss.at[c], gc_rs.at[c], other)

    def image_sums(c):
        at = slice(c * CC, (c + 1) * CC)
        for b in range(2):
            rows = slice(b * S // 2, (b + 1) * S // 2)
            g = dot3(d_hi[:, rows], d_lo[:, rows], yb_hi[:, at], yb_lo[:, at], 0, 0)
            for i in range(NL):
                r = ORDER[b * 2 + i // 2]
                for j in range(NX):
                    gxs[c, i % 2, j, r] = g[i * GROUP + j * SHARE : i * GROUP + (j + 1) * SHARE, :]
        gcopy(c).start()

    def ahead(d):
        return lax.rem(x + d, NX)

    def xa(c, right):
        b = 0 if right else 1
        i = c * 2 + b
        src = gxs.at[c, 0, ahead(2), pl.ds(b * 2, 2)]
        return rcopy(src, xa_in.at[i], xa_ss.at[i], xa_rs.at[i], at_x(1 if right else NX - 1))

    def xf(c, right):
        d = 1 if right else NX - 1
        i = c * 2 + (0 if right else 1)
        return rcopy(gxs.at[c, 0, ahead(d)], xf_in.at[i], xf_ss.at[i], xf_rs.at[i], at_x(d))

    def core_done(c):
        gcopy(c).wait()
        for j in range(NX):
            gxs[c, 0, j] = gxs[c, 0, j] + gc_in[c, j]
        for right in (True, False):
            xa(c, right).start()

    def xa_done(c):
        for right in (True, False):
            xa(c, right).wait()
            d = 1 if right else NX - 1
            b = 0 if right else 1
            for i in range(2):
                r = b * 2 + i
                gxs[c, 0, ahead(d), r] = gxs[c, 0, ahead(d), r] + xa_in[c * 2 + b, i]
            xf(c, right).start()

    def q(c, r):
        i = c * 3 + r - 1
        return rcopy(zs.at[c, r], zr.at[c, r - 1], q_ss.at[i], q_rs.at[i], at_line(r))

    def xf_done(c):
        for right in (True, False):
            xf(c, right).wait()
        zs[c] = gxs[c, 0, x] + xf_in[c * 2] + xf_in[c * 2 + 1]
        for r in (2, 1, 3):
            q(c, r).start()

    image_sums(0)
    image_sums(1)
    text_sums(1)
    rs_start()
    core_done(0)
    image_sums(2)
    core_done(1)
    text_sums(0)
    lx[x] = lsum(lc, lcopies, 2)
    lcopies = lsend(lx, x, lx_ss, lx_rs, at_x, NX)
    core_done(2)
    xa_done(0)
    rs_take(1)
    xa_done(1)
    xa_done(2)
    ly[y] = lsum(lx, lcopies, NX)
    lcopies = lsend(ly, y, ly_ss, ly_rs, at_y, NY)
    rs_take(2)
    xf_done(0)
    xf_done(1)
    rs_take(3)
    lz[z] = lsum(ly, lcopies, NY)
    lcopies = lsend(lz, z, lz_ss, lz_rs, lambda d: at_z(z + d), NZ)
    xf_done(2)
    rs_take(4)
    gz[0] = gy[SLOT[0] * TEXT : SLOT[0] * TEXT + SHARE, :]
    gz[1] = gy[SLOT[0] * TEXT + SHARE : (SLOT[0] + 1) * TEXT, :]
    hcopy = rcopy(gz.at[1 - zh], gz_in, h_ss, h_rs, at_z(z + NL))
    hcopy.start()
    loss = lsum(lz, lcopies, NZ) * (1.0 / (float(N) * float(N)))
    loss_o[0] = loss[0, 0]

    for c in range(NC):
        for r in range(1, NL):
            q(c, r).wait()
        gx[:, c * CC : (c + 1) * CC] = zs[c, 0] + zr[c, 0] + zr[c, 1] + zr[c, 2]
    g = scale1 * (gx[...] - y_own)
    gi_o[...] = inv_x * (g - x_own * jnp.sum(x_own * g, axis=-1, keepdims=True))

    hcopy.wait()
    g = scale1 * (gz[zh] + gz_in[...] - x_own)
    gt_o[...] = iy_own * (g - y_own * jnp.sum(y_own * g, axis=-1, keepdims=True))

    rcopy(gy.at[sent, :], gy.at[sent, :], rs_ss, rs_rs.at[0], other).wait_send()


def local(image, text, log_temp, bias):
    vmem = pl.BlockSpec(memory_space=pltpu.VMEM)
    smem = pl.BlockSpec(memory_space=pltpu.SMEM)
    hbm = pl.BlockSpec(memory_space=pl.ANY)
    dma = pltpu.SemaphoreType.DMA
    scratch = [
        pltpu.VMEM((BLOCK, D), F32),
        pltpu.VMEM((TEXT, D), F32),
        pltpu.VMEM((2, GROUP, D), F32),
        pltpu.VMEM((TEXT, D), F32),
        pltpu.VMEM((NL - 1, GROUP, D), F32),
        pltpu.VMEM((NL, GROUP, D), F32),
        pltpu.VMEM((T, D), F32),
        pltpu.VMEM((S, D), BF16),
        pltpu.VMEM((S, D), BF16),
        pltpu.VMEM((T, D), BF16),
        pltpu.VMEM((T, D), BF16),
        pltpu.VMEM((T, S), BF16),
        pltpu.VMEM((T, S), BF16),
        pltpu.VMEM((T, D), F32),
        pltpu.VMEM((8 * LANES, TEXT, LW), F32),
        pltpu.VMEM((2, SHARE, D), F32),
        pltpu.VMEM((SHARE, D), F32),
        pltpu.VMEM((NC, 2, NX, NL, SHARE, CC), F32),
        pltpu.VMEM((NC, NX, NL, SHARE, CC), F32),
        pltpu.VMEM((2 * NC, 2, SHARE, CC), F32),
        pltpu.VMEM((2 * NC, NL, SHARE, CC), F32),
        pltpu.VMEM((NC, NL, SHARE, CC), F32),
        pltpu.VMEM((NC, NL - 1, SHARE, CC), F32),
        pltpu.VMEM((SHARE, D), F32),
        pltpu.VMEM((8, S // 2), F32),
        pltpu.VMEM((2, 8, 128), F32),
        pltpu.VMEM((NX, 8, 128), F32),
        pltpu.VMEM((NY, 8, 128), F32),
        pltpu.VMEM((NZ, 8, 128), F32),
        dma((2,)),
    ]
    scratch += [dma, dma((8 * LANES,))]
    for n in (10, 3, 6):
        scratch += [dma((n,)), dma((n,))]
    scratch += [dma, dma((8 * LANES,))]
    for n in (NC, 2 * NC, 2 * NC, 3 * NC):
        scratch += [dma((n,)), dma((n,))]
    scratch += [dma, dma]
    for n in (1, NX - 1, NY - 1, NZ - 1):
        scratch += [dma((n,)), dma((n,))]
    loss, gi, gt = pl.pallas_call(
        kernel,
        out_shape=(
            jax.ShapeDtypeStruct((1,), F32),
            jax.ShapeDtypeStruct((SHARE, D), F32),
            jax.ShapeDtypeStruct((SHARE, D), F32),
        ),
        in_specs=[hbm, hbm, smem, smem],
        out_specs=(smem, vmem, vmem),
        scratch_shapes=scratch,
        compiler_params=pltpu.CompilerParams(
            collective_id=0, has_side_effects=True, vmem_limit_bytes=56 << 20
        ),
    )(image, text, log_temp, bias)
    return loss[0], gi, gt


def solution(mesh):
    in_specs = (P("dp", None), P("dp", None), P(), P())
    out_specs = (P(), P(("dp", "split"), None), P(("dp", "split"), None))
    return jax.shard_map(local, mesh=mesh, in_specs=in_specs, out_specs=out_specs, check_vma=False)
```

```python
import jax
import jax.numpy as jnp
from jax import lax
from jax.experimental import pallas as pl
from jax.experimental.pallas import tpu as pltpu
from jax.sharding import PartitionSpec as P

EPS = 1e-06
MESH = pl.DeviceIdType.MESH
D = 768
NX, NY, NZ, NL = 4, 8, 8, 4
N = 14336
SHARE = 28
BLOCK = 224
TEXT = 56
GROUP = NX * SHARE
S = 2 * NL * GROUP
ORDER = (0, 1, 3, 2)
T = NY * TEXT
HALF = D // 2
NC = 3
CC = D // NC
LANES = 3
LW = D // LANES
TT = T // 2
F32 = jnp.float32
BF16 = jnp.bfloat16
SLOT = {1: 0, 7: 1, 2: 2, 6: 3, 3: 4, 5: 5, 0: 6, 4: 7}


def split_bf16(v):
    hi = v.astype(BF16)
    return hi, (v - hi.astype(F32)).astype(BF16)


def dot3(ah, al, bh, bl, ca, cb):
    def one(a, b):
        return lax.dot_general(a, b, (((ca,), (cb,)), ((), ())), preferred_element_type=F32)

    return one(ah, bh) + one(al, bh) + one(ah, bl)


def unit_rows(v):
    inv = lax.rsqrt(jnp.sum(v * v, axis=-1, keepdims=True) + EPS)
    return v * inv, inv


def kernel(
    img_hbm, txt_hbm, lt_ref, bias_ref,
    loss_o, g_o,
    img, txt, xo, yo, xs, xc, ys, xb_hi, xb_lo, yb_hi, yb_lo, d_hi, d_lo,
    gy, rs_in, gz, gz_in, gxs, gc_in, xa_in, xf_in, zs, zr, gx, lacc, lc, lx, ly, lz,
    in_s, ag_ss, ag_rs, ic_ss, ic_rs, iz_ss, iz_rs, ix_ss, ix_rs,
    rs_ss, rs_rs, gc_ss, gc_rs, xa_ss, xa_rs, xf_ss, xf_rs, q_ss, q_rs, h_ss, h_rs,
    lc_ss, lc_rs, lx_ss, lx_rs, ly_ss, ly_rs, lz_ss, lz_rs,
):
    dp = lax.axis_index("dp")
    split = lax.axis_index("split")
    k = lax.rem(dp, 2)
    y = lax.rem(lax.div(dp, 2), NY)
    zl = lax.div(dp, 2 * NY)
    x = lax.div(split, 2)
    zh = lax.rem(split, 2)
    z = zh * NL + zl
    def dev(x_, y_, z_, k_):
        return (lax.rem(z_, NL) * (2 * NY) + y_ * 2 + k_, x_ * 2 + lax.div(z_, NL))

    def at_x(d):
        return dev(lax.rem(x + d, NX), y, z, k)

    def at_y(d):
        return dev(x, lax.rem(y + d, NY), z, k)

    def at_z(z_):
        return dev(x, y, lax.rem(z_, NZ), k)

    def at_line(r):
        return dev(x, y, zh * NL + lax.rem(zl + r, NL), k)

    other = dev(x, y, z, 1 - k)

    def rcopy(src, dst, ss, rs, to):
        return pltpu.make_async_remote_copy(src, dst, ss, rs, device_id=to, device_id_type=MESH)

    own_rows = pl.ds(pl.multiple_of(x * TEXT, 8), TEXT)
    in_img = pltpu.make_async_copy(img_hbm, img, in_s.at[0])
    in_txt = pltpu.make_async_copy(txt_hbm.at[own_rows, :], txt, in_s.at[1])
    in_txt.start()
    in_img.start()
    barrier = pltpu.get_barrier_semaphore()
    partners = [at_x(d) for d in range(1, NX)] + [at_y(d) for d in range(1, NY)]
    partners += [at_z(z + d) for d in range(1, NZ)] + [other]
    for to in partners:
        pl.semaphore_signal(barrier, inc=1, device_id=to, device_id_type=MESH)

    def trow(dy):
        return pl.ds(SLOT[dy] * TEXT, TEXT)

    in_txt.wait()
    y_unit, inv_y = unit_rows(txt[...])
    yo[...] = y_unit
    ys[trow(0), :] = y_unit
    pl.semaphore_wait(barrier, len(partners))

    def lane_cols(n):
        return pl.ds(n * LW, LW)

    def steps(n, right):
        return NY // 2 if right == (n % 2 == 0) else NY // 2 - 1

    def ag(n, right, s):
        if right:
            src, dst, to = (NY - (s - 1)) % NY, NY - s, at_y(1)
        else:
            src, dst, to = s - 1, s, at_y(NY - 1)
        i = n * 8 + (0 if right else 4) + s - 1
        return rcopy(ys.at[trow(src), lane_cols(n)], ys.at[trow(dst), lane_cols(n)], ag_ss, ag_rs.at[i], to)

    for n in range(LANES):
        for right in (True, False):
            ag(n, right, 1).start()

    in_img.wait()
    unit = unit_rows(img[...])[0]
    for i in range(2 * NX):
        xo[i % 2, i // 2 * SHARE : (i // 2 + 1) * SHARE, :] = unit[i * SHARE : (i + 1) * SHARE, :]

    hx = lax.rem(x, 2)

    def half(h):
        return pl.ds(pl.multiple_of(h * HALF, 128), HALF)

    def img_z(r):
        z_ = z + {1: NZ - 1, 3: 1}[r] if r != 2 else z + 2 + NL * k
        there = lax.div(lax.rem(z_, NZ), NL)
        return rcopy(xo.at[there, :, half(hx)], xs.at[r - 1, :, half(hx)], iz_ss.at[r - 1], iz_rs.at[r - 1], at_z(z_))

    def img_x(r, right):
        i = (r - 1) * 2 + (0 if right else 1)
        ref = xs.at[r - 1, pl.ds(0 if right else GROUP // 2, GROUP // 2), half(hx)]
        return rcopy(ref, ref, ix_ss.at[i], ix_rs.at[i], at_x(1 if right else NX - 1))

    def core_z(r):
        return rcopy(xs.at[r - 1, :, half(hx)], xc.at[r, :, half(hx)], ic_ss.at[r], ic_rs.at[r], other)

    def core_x(r, right):
        i = NL + (r - 1) * 2 + (0 if right else 1)
        rows = pl.ds(0 if right else GROUP // 2, GROUP // 2)
        src = xs.at[r - 1, rows, half(1 - hx)]
        return rcopy(src, xc.at[r, rows, half(1 - hx)], ic_ss.at[i], ic_rs.at[i], other)

    core_own = rcopy(xo.at[zh], xc.at[0], ic_ss.at[0], ic_rs.at[0], other)
    for r in (1, 3, 2):
        img_z(r).start()
    core_own.start()

    def from_z(r):
        img_z(r).wait()
        for right in (True, False):
            img_x(r, right).start()
        core_z(r).start()

    def from_x(r):
        for right in (True, False):
            img_x(r, right).wait()
            core_x(r, right).start()

    def from_core(r):
        core_z(r).wait()
        for right in (True, False):
            core_x(r, right).wait()

    def put_image(r, block, kk):
        g = ORDER.index(r) * 2 + kk
        rows = slice(g * GROUP, (g + 1) * GROUP)
        hi, lo = split_bf16(block)
        xb_hi[rows, :] = hi
        xb_lo[rows, :] = lo

    def put_text(c):
        rows = slice(c * 2 * TEXT, (c + 1) * 2 * TEXT)
        hi, lo = split_bf16(ys[rows, :])
        yb_hi[rows, :] = hi
        yb_lo[rows, :] = lo

    put_image(0, xo[zh], 0)

    scale = jnp.exp(jnp.full((1, S // 2), lt_ref[0], F32))
    offset = bias_ref[0]
    lacc[...] = jnp.zeros_like(lacc)

    def pairs(t, half):
        rows = slice(t * TT, (t + 1) * TT)
        at = slice(half * S // 2, (half + 1) * S // 2)
        prod = dot3(yb_hi[rows, :], yb_lo[rows, :], xb_hi[at, :], xb_lo[at, :], 1, 1)
        logits = scale * prod + offset
        u = jnp.exp(-jnp.abs(logits))
        w = 1.0 + u
        r = 1.0 / w
        sp = jnp.maximum(logits, 0.0) + (jnp.log(w) + (u - (w - 1.0)) * r)
        sig = jnp.where(logits >= 0.0, r, u * r)
        lacc[...] += jnp.sum(sp.reshape(TT // 8, 8, S // 2), axis=0)
        hi, lo = split_bf16(sig)
        d_hi[rows, at] = hi
        d_lo[rows, at] = lo

    def text_sums(t):
        rows = slice(t * TT, (t + 1) * TT)
        gy[rows, :] = dot3(d_hi[rows, :], d_lo[rows, :], xb_hi[...], xb_lo[...], 1, 0)

    def ag_take(s):
        for n in range(LANES):
            for right in (True, False):
                if s <= steps(n, right):
                    ag(n, right, s).wait_recv()
                    if s < steps(n, right):
                        ag(n, right, s + 1).start()

    ag_take(1)
    core_own.wait()
    put_image(0, xc[0], 1)
    from_z(1)
    from_z(3)
    put_text(0)
    ag_take(2)
    put_text(1)
    from_z(2)
    ag_take(3)
    put_text(2)
    from_x(1)
    from_x(3)
    put_image(1, xs[0], 0)
    put_image(3, xs[2], 0)
    from_core(1)
    put_image(1, xc[1], 1)
    pairs(0, 0)
    from_x(2)
    from_core(3)
    put_image(3, xc[3], 1)
    put_image(2, xs[1], 0)
    from_core(2)
    put_image(2, xc[2], 1)
    pairs(0, 1)
    ag_take(4)
    put_text(3)
    pairs(1, 0)
    pairs(1, 1)

    sent = pl.ds(0, (NY - 1) * TEXT)
    rcopy(ys.at[sent, :], ys.at[sent, :], ag_ss, ag_rs.at[0], other).wait_send()

    raw = img[0:SHARE, :]
    for i in range(1, 2 * NX):
        raw = jnp.where(split == i, img[i * SHARE : (i + 1) * SHARE, :], raw)
    x_own, inv_x = unit_rows(raw)
    y_both = yo[...]
    y_own = jnp.where(zh == 0, y_both[0:SHARE, :], y_both[SHARE:TEXT, :])
    iy_own = jnp.where(zh == 0, inv_y[0:SHARE, :], inv_y[SHARE:TEXT, :])
    scale1 = scale[:, 0:1]
    same = jnp.sum(jnp.sum(x_own * y_own, axis=-1, keepdims=True) * scale1 + offset)
    ly[y] = jnp.full((8, 128), jnp.sum(lacc[...]) - same, F32)

    def lsend(buf, me, ss, rs, to, n):
        copies = [rcopy(buf.at[me], buf.at[me], ss.at[d - 1], rs.at[d - 1], to(d)) for d in range(1, n)]
        for c in copies:
            c.start()
        return copies

    def lsum(buf, copies, n):
        for c in copies:
            c.wait()
        out = buf[0]
        for i in range(1, n):
            out = out + buf[i]
        return out

    lcopies = lsend(ly, y, ly_ss, ly_rs, at_y, NY)

    def rs_unit(n, right, s):
        dist = steps(n, right) - s + 1
        return dist if right or dist == 0 else NY - dist

    def rs(n, right, s):
        i = n * 8 + (0 if right else 4) + s - 1
        to = at_y(1 if right else NY - 1)
        src = gy.at[trow(rs_unit(n, right, s)), lane_cols(n)]
        return rcopy(src, rs_in.at[i], rs_ss, rs_rs.at[i], to)

    def rs_start():
        for n in range(LANES):
            for right in (True, False):
                rs(n, right, 1).start()

    def rs_take(s):
        for n in range(LANES):
            for right in (True, False):
                if s <= steps(n, right):
                    rs(n, right, s).wait_recv()
                    i = n * 8 + (0 if right else 4) + s - 1
                    unit = rs_unit(n, right, s + 1)
                    at = slice(SLOT[unit] * TEXT, (SLOT[unit] + 1) * TEXT), slice(n * LW, (n + 1) * LW)
                    gy[at] = gy[at] + rs_in[i]
                    if s < steps(n, right):
                        rs(n, right, s + 1).start()

    def gcopy(c):
        return rcopy(gxs.at[c, 1], gc_in.at[c], gc_ss.at[c], gc_rs.at[c], other)

    def image_sums(c):
        at = slice(c * CC, (c + 1) * CC)
        for b in range(2):
            rows = slice(b * S // 2, (b + 1) * S // 2)
            g = dot3(d_hi[:, rows], d_lo[:, rows], yb_hi[:, at], yb_lo[:, at], 0, 0)
            for i in range(NL):
                r = ORDER[b * 2 + i // 2]
                for j in range(NX):
                    gxs[c, i % 2, j, r] = g[i * GROUP + j * SHARE : i * GROUP + (j + 1) * SHARE, :]
        gcopy(c).start()

    def ahead(d):
        return lax.rem(x + d, NX)

    def xa(c, right):
        b = 0 if right else 1
        i = c * 2 + b
        src = gxs.at[c, 0, ahead(2), pl.ds(b * 2, 2)]
        return rcopy(src, xa_in.at[i], xa_ss.at[i], xa_rs.at[i], at_x(1 if right else NX - 1))

    def xf(c, right):
        d = 1 if right else NX - 1
        i = c * 2 + (0 if right else 1)
        return rcopy(gxs.at[c, 0, ahead(d)], xf_in.at[i], xf_ss.at[i], xf_rs.at[i], at_x(d))

    def core_done(c):
        gcopy(c).wait()
        for j in range(NX):
            gxs[c, 0, j] = gxs[c, 0, j] + gc_in[c, j]
        for right in (True, False):
            xa(c, right).start()

    def xa_done(c):
        for right in (True, False):
            xa(c, right).wait()
            d = 1 if right else NX - 1
            b = 0 if right else 1
            for i in range(2):
                r = b * 2 + i
                gxs[c, 0, ahead(d), r] = gxs[c, 0, ahead(d), r] + xa_in[c * 2 + b, i]
            xf(c, right).start()

    def q(c, r):
        i = c * 3 + r - 1
        return rcopy(zs.at[c, r], zr.at[c, r - 1], q_ss.at[i], q_rs.at[i], at_line(r))

    def xf_done(c):
        for right in (True, False):
            xf(c, right).wait()
        zs[c] = gxs[c, 0, x] + xf_in[c * 2] + xf_in[c * 2 + 1]
        for r in (2, 1, 3):
            q(c, r).start()

    image_sums(0)
    image_sums(1)
    text_sums(1)
    rs_start()
    core_done(0)
    image_sums(2)
    core_done(1)
    text_sums(0)
    lz[z] = lsum(ly, lcopies, NY)
    lcopies = lsend(lz, z, lz_ss, lz_rs, lambda d: at_z(z + d), NZ)
    core_done(2)
    xa_done(0)
    rs_take(1)
    xa_done(1)
    xa_done(2)
    rs_take(2)
    lc[k] = lsum(lz, lcopies, NZ)
    lcopies = lsend(lc, k, lc_ss, lc_rs, lambda d: other, 2)
    xf_done(0)
    lx[x] = lsum(lc, lcopies, 2)
    lcopies = lsend(lx, x, lx_ss, lx_rs, at_x, NX)
    xf_done(1)
    rs_take(3)
    xf_done(2)
    rs_take(4)
    gz[0] = gy[SLOT[0] * TEXT : SLOT[0] * TEXT + SHARE, :]
    gz[1] = gy[SLOT[0] * TEXT + SHARE : (SLOT[0] + 1) * TEXT, :]
    hcopy = rcopy(gz.at[1 - zh], gz_in, h_ss, h_rs, at_z(z + NL))
    hcopy.start()
    loss = lsum(lx, lcopies, NX) * (1.0 / (float(N) * float(N)))
    loss_o[0] = loss[0, 0]

    for c in range(NC):
        for r in range(1, NL):
            q(c, r).wait()
        gx[:, c * CC : (c + 1) * CC] = zs[c, 0] + zr[c, 0] + zr[c, 1] + zr[c, 2]
    g = scale1 * (gx[...] - y_own)
    g_o[0] = inv_x * (g - x_own * jnp.sum(x_own * g, axis=-1, keepdims=True))

    hcopy.wait()
    g = scale1 * (gz[zh] + gz_in[...] - x_own)
    g_o[1] = iy_own * (g - y_own * jnp.sum(y_own * g, axis=-1, keepdims=True))

    rcopy(gy.at[sent, :], gy.at[sent, :], rs_ss, rs_rs.at[0], other).wait_send()


def local(image, text, log_temp, bias):
    vmem = pl.BlockSpec(memory_space=pltpu.VMEM)
    smem = pl.BlockSpec(memory_space=pltpu.SMEM)
    hbm = pl.BlockSpec(memory_space=pl.ANY)
    dma = pltpu.SemaphoreType.DMA
    scratch = [
        pltpu.VMEM((BLOCK, D), F32),
        pltpu.VMEM((TEXT, D), F32),
        pltpu.VMEM((2, GROUP, D), F32),
        pltpu.VMEM((TEXT, D), F32),
        pltpu.VMEM((NL - 1, GROUP, D), F32),
        pltpu.VMEM((NL, GROUP, D), F32),
        pltpu.VMEM((T, D), F32),
        pltpu.VMEM((S, D), BF16),
        pltpu.VMEM((S, D), BF16),
        pltpu.VMEM((T, D), BF16),
        pltpu.VMEM((T, D), BF16),
        pltpu.VMEM((T, S), BF16),
        pltpu.VMEM((T, S), BF16),
        pltpu.VMEM((T, D), F32),
        pltpu.VMEM((8 * LANES, TEXT, LW), F32),
        pltpu.VMEM((2, SHARE, D), F32),
        pltpu.VMEM((SHARE, D), F32),
        pltpu.VMEM((NC, 2, NX, NL, SHARE, CC), F32),
        pltpu.VMEM((NC, NX, NL, SHARE, CC), F32),
        pltpu.VMEM((2 * NC, 2, SHARE, CC), F32),
        pltpu.VMEM((2 * NC, NL, SHARE, CC), F32),
        pltpu.VMEM((NC, NL, SHARE, CC), F32),
        pltpu.VMEM((NC, NL - 1, SHARE, CC), F32),
        pltpu.VMEM((SHARE, D), F32),
        pltpu.VMEM((8, S // 2), F32),
        pltpu.VMEM((2, 8, 128), F32),
        pltpu.VMEM((NX, 8, 128), F32),
        pltpu.VMEM((NY, 8, 128), F32),
        pltpu.VMEM((NZ, 8, 128), F32),
        dma((2,)),
    ]
    scratch += [dma, dma((8 * LANES,))]
    for n in (10, 3, 6):
        scratch += [dma((n,)), dma((n,))]
    scratch += [dma, dma((8 * LANES,))]
    for n in (NC, 2 * NC, 2 * NC, 3 * NC):
        scratch += [dma((n,)), dma((n,))]
    scratch += [dma, dma]
    for n in (1, NX - 1, NY - 1, NZ - 1):
        scratch += [dma((n,)), dma((n,))]
    loss, g = pl.pallas_call(
        kernel,
        out_shape=(
            jax.ShapeDtypeStruct((1,), F32),
            jax.ShapeDtypeStruct((2, SHARE, D), F32),
        ),
        in_specs=[hbm, hbm, smem, smem],
        out_specs=(smem, vmem),
        scratch_shapes=scratch,
        compiler_params=pltpu.CompilerParams(
            collective_id=0, has_side_effects=True, vmem_limit_bytes=56 << 20
        ),
    )(image, text, log_temp, bias)
    return loss[0], g[0], g[1]


def solution(mesh):
    in_specs = (P("dp", None), P("dp", None), P(), P())
    out_specs = (P(), P(("dp", "split"), None), P(("dp", "split"), None))
    return jax.shard_map(local, mesh=mesh, in_specs=in_specs, out_specs=out_specs, check_vma=False)
```

```python
import jax
import jax.numpy as jnp
from jax import lax
from jax.experimental import pallas as pl
from jax.experimental.pallas import tpu as pltpu
from jax.sharding import PartitionSpec as P

EPS = 1e-06
MESH = pl.DeviceIdType.MESH
D = 768
NX, NY, NZ, NL = 4, 8, 8, 4
N = 14336
SHARE = 28
BLOCK = 224
TEXT = 56
GROUP = NX * SHARE
S = 2 * NL * GROUP
ORDER = (0, 1, 3, 2)
T = NY * TEXT
HALF = D // 2
NC = 3
CC = D // NC
LANES = 3
LW = D // LANES
TT = T // 2
F32 = jnp.float32
BF16 = jnp.bfloat16
SLOT = {1: 0, 7: 1, 2: 2, 6: 3, 3: 4, 5: 5, 0: 6, 4: 7}


def split_bf16(v):
    hi = v.astype(BF16)
    return hi, (v - hi.astype(F32)).astype(BF16)


def dot3(ah, al, bh, bl, ca, cb):
    def one(a, b):
        return lax.dot_general(a, b, (((ca,), (cb,)), ((), ())), preferred_element_type=F32)

    return one(ah, bh) + one(al, bh) + one(ah, bl)


def unit_rows(v):
    inv = lax.rsqrt(jnp.sum(v * v, axis=-1, keepdims=True) + EPS)
    return v * inv, inv


def kernel(
    img_hbm, txt_hbm, lt_ref, bias_ref,
    loss_o, g_o,
    img, txt, xo, yo, xs, xc, ys, xb_hi, xb_lo, yb_hi, yb_lo, d_hi, d_lo,
    gy, rs_in, gz, gz_in, gxs, gc_in, xa_in, xf_in, zs, zr, gx, lacc, lc, lx, ly, lz,
    in_s, ag_ss, ag_rs, ic_ss, ic_rs, iz_ss, iz_rs, ix_ss, ix_rs,
    rs_ss, rs_rs, gc_ss, gc_rs, xa_ss, xa_rs, xf_ss, xf_rs, q_ss, q_rs, h_ss, h_rs,
    lc_ss, lc_rs, lx_ss, lx_rs, ly_ss, ly_rs, lz_ss, lz_rs,
):
    dp = lax.axis_index("dp")
    split = lax.axis_index("split")
    k = lax.rem(dp, 2)
    y = lax.rem(lax.div(dp, 2), NY)
    zl = lax.div(dp, 2 * NY)
    x = lax.div(split, 2)
    zh = lax.rem(split, 2)
    z = zh * NL + zl
    def dev(x_, y_, z_, k_):
        return (lax.rem(z_, NL) * (2 * NY) + y_ * 2 + k_, x_ * 2 + lax.div(z_, NL))

    def at_x(d):
        return dev(lax.rem(x + d, NX), y, z, k)

    def at_y(d):
        return dev(x, lax.rem(y + d, NY), z, k)

    def at_z(z_):
        return dev(x, y, lax.rem(z_, NZ), k)

    def at_line(r):
        return dev(x, y, zh * NL + lax.rem(zl + r, NL), k)

    other = dev(x, y, z, 1 - k)

    def rcopy(src, dst, ss, rs, to):
        return pltpu.make_async_remote_copy(src, dst, ss, rs, device_id=to, device_id_type=MESH)

    own_rows = pl.ds(pl.multiple_of(x * TEXT, 8), TEXT)
    in_img = pltpu.make_async_copy(img_hbm, img, in_s.at[0])
    in_txt = pltpu.make_async_copy(txt_hbm.at[own_rows, :], txt, in_s.at[1])
    in_txt.start()
    in_img.start()
    barrier = pltpu.get_barrier_semaphore()
    partners = [at_x(d) for d in range(1, NX)] + [at_y(d) for d in range(1, NY)]
    partners += [at_z(z + d) for d in range(1, NZ)] + [other]
    for to in partners:
        pl.semaphore_signal(barrier, inc=1, device_id=to, device_id_type=MESH)

    def trow(dy):
        return pl.ds(SLOT[dy] * TEXT, TEXT)

    in_txt.wait()
    y_unit, inv_y = unit_rows(txt[...])
    yo[...] = y_unit
    ys[trow(0), :] = y_unit
    pl.semaphore_wait(barrier, len(partners))

    def lane_cols(n):
        return pl.ds(n * LW, LW)

    def steps(n, right):
        return NY // 2 if right == (n % 2 == 0) else NY // 2 - 1

    def ag(n, right, s):
        if right:
            src, dst, to = (NY - (s - 1)) % NY, NY - s, at_y(1)
        else:
            src, dst, to = s - 1, s, at_y(NY - 1)
        i = n * 8 + (0 if right else 4) + s - 1
        return rcopy(ys.at[trow(src), lane_cols(n)], ys.at[trow(dst), lane_cols(n)], ag_ss, ag_rs.at[i], to)

    for n in range(LANES):
        for right in (True, False):
            ag(n, right, 1).start()

    in_img.wait()
    unit = unit_rows(img[...])[0]
    for i in range(2 * NX):
        xo[i % 2, i // 2 * SHARE : (i // 2 + 1) * SHARE, :] = unit[i * SHARE : (i + 1) * SHARE, :]

    hx = lax.rem(x, 2)

    def half(h):
        return pl.ds(pl.multiple_of(h * HALF, 128), HALF)

    def img_z(r):
        z_ = z + {1: NZ - 1, 3: 1}[r] if r != 2 else z + 2 + NL * k
        there = lax.div(lax.rem(z_, NZ), NL)
        return rcopy(xo.at[there, :, half(hx)], xs.at[r - 1, :, half(hx)], iz_ss.at[r - 1], iz_rs.at[r - 1], at_z(z_))

    def img_x(r, right):
        i = (r - 1) * 2 + (0 if right else 1)
        ref = xs.at[r - 1, pl.ds(0 if right else GROUP // 2, GROUP // 2), half(hx)]
        return rcopy(ref, ref, ix_ss.at[i], ix_rs.at[i], at_x(1 if right else NX - 1))

    def core_z(r):
        return rcopy(xs.at[r - 1, :, half(hx)], xc.at[r, :, half(hx)], ic_ss.at[r], ic_rs.at[r], other)

    def core_x(r, right):
        i = NL + (r - 1) * 2 + (0 if right else 1)
        rows = pl.ds(0 if right else GROUP // 2, GROUP // 2)
        src = xs.at[r - 1, rows, half(1 - hx)]
        return rcopy(src, xc.at[r, rows, half(1 - hx)], ic_ss.at[i], ic_rs.at[i], other)

    core_own = rcopy(xo.at[zh], xc.at[0], ic_ss.at[0], ic_rs.at[0], other)
    for r in (1, 3, 2):
        img_z(r).start()
    core_own.start()

    def from_z(r):
        img_z(r).wait()
        for right in (True, False):
            img_x(r, right).start()
        core_z(r).start()

    def from_x(r):
        for right in (True, False):
            img_x(r, right).wait()
            core_x(r, right).start()

    def from_core(r):
        core_z(r).wait()
        for right in (True, False):
            core_x(r, right).wait()

    def put_image(r, block, kk):
        g = ORDER.index(r) * 2 + kk
        rows = slice(g * GROUP, (g + 1) * GROUP)
        hi, lo = split_bf16(block)
        xb_hi[rows, :] = hi
        xb_lo[rows, :] = lo

    def put_text(c):
        rows = slice(c * 2 * TEXT, (c + 1) * 2 * TEXT)
        hi, lo = split_bf16(ys[rows, :])
        yb_hi[rows, :] = hi
        yb_lo[rows, :] = lo

    put_image(0, xo[zh], 0)

    scale = jnp.exp(jnp.full((1, S // 2), lt_ref[0], F32))
    offset = bias_ref[0]
    lacc[...] = jnp.zeros_like(lacc)

    def pairs(start, n, half):
        rows = slice(start, start + n)
        at = slice(half * S // 2, (half + 1) * S // 2)
        prod = dot3(yb_hi[rows, :], yb_lo[rows, :], xb_hi[at, :], xb_lo[at, :], 1, 1)
        logits = scale * prod + offset
        u = jnp.exp(-jnp.abs(logits))
        w = 1.0 + u
        r = 1.0 / w
        sp = jnp.maximum(logits, 0.0) + (jnp.log(w) + (u - (w - 1.0)) * r)
        sig = jnp.where(logits >= 0.0, r, u * r)
        lacc[...] += jnp.sum(sp.reshape(n // 8, 8, S // 2), axis=0)
        hi, lo = split_bf16(sig)
        d_hi[rows, at] = hi
        d_lo[rows, at] = lo

    def text_sums(t):
        rows = slice(t * TT, (t + 1) * TT)
        gy[rows, :] = dot3(d_hi[rows, :], d_lo[rows, :], xb_hi[...], xb_lo[...], 1, 0)

    def ag_take(s):
        for n in range(LANES):
            for right in (True, False):
                if s <= steps(n, right):
                    ag(n, right, s).wait_recv()
                    if s < steps(n, right):
                        ag(n, right, s + 1).start()

    ag_take(1)
    core_own.wait()
    put_image(0, xc[0], 1)
    from_z(1)
    from_z(3)
    put_text(0)
    ag_take(2)
    put_text(1)
    from_z(2)
    ag_take(3)
    put_text(2)
    from_x(1)
    from_x(3)
    put_image(1, xs[0], 0)
    put_image(3, xs[2], 0)
    from_core(1)
    put_image(1, xc[1], 1)
    pairs(0, TT, 0)
    from_x(2)
    from_core(3)
    put_image(3, xc[3], 1)
    put_image(2, xs[1], 0)
    from_core(2)
    put_image(2, xc[2], 1)
    pairs(0, TT, 1)
    for b in range(2):
        pairs(TT, TT // 2, b)
    ag_take(4)
    put_text(3)
    for b in range(2):
        pairs(TT + TT // 2, TT // 2, b)

    sent = pl.ds(0, (NY - 1) * TEXT)
    rcopy(ys.at[sent, :], ys.at[sent, :], ag_ss, ag_rs.at[0], other).wait_send()

    raw = img[0:SHARE, :]
    for i in range(1, 2 * NX):
        raw = jnp.where(split == i, img[i * SHARE : (i + 1) * SHARE, :], raw)
    x_own, inv_x = unit_rows(raw)
    y_both = yo[...]
    y_own = jnp.where(zh == 0, y_both[0:SHARE, :], y_both[SHARE:TEXT, :])
    iy_own = jnp.where(zh == 0, inv_y[0:SHARE, :], inv_y[SHARE:TEXT, :])
    scale1 = scale[:, 0:1]
    same = jnp.sum(jnp.sum(x_own * y_own, axis=-1, keepdims=True) * scale1 + offset)
    ly[y] = jnp.full((8, 128), jnp.sum(lacc[...]) - same, F32)

    def lsend(buf, me, ss, rs, to, n):
        copies = [rcopy(buf.at[me], buf.at[me], ss.at[d - 1], rs.at[d - 1], to(d)) for d in range(1, n)]
        for c in copies:
            c.start()
        return copies

    def lsum(buf, copies, n):
        for c in copies:
            c.wait()
        out = buf[0]
        for i in range(1, n):
            out = out + buf[i]
        return out

    lcopies = lsend(ly, y, ly_ss, ly_rs, at_y, NY)

    def rs_unit(n, right, s):
        dist = steps(n, right) - s + 1
        return dist if right or dist == 0 else NY - dist

    def rs(n, right, s):
        i = n * 8 + (0 if right else 4) + s - 1
        to = at_y(1 if right else NY - 1)
        src = gy.at[trow(rs_unit(n, right, s)), lane_cols(n)]
        return rcopy(src, rs_in.at[i], rs_ss, rs_rs.at[i], to)

    def rs_start():
        for n in range(LANES):
            for right in (True, False):
                rs(n, right, 1).start()

    def rs_take(s):
        for n in range(LANES):
            for right in (True, False):
                if s <= steps(n, right):
                    rs(n, right, s).wait_recv()
                    i = n * 8 + (0 if right else 4) + s - 1
                    unit = rs_unit(n, right, s + 1)
                    at = slice(SLOT[unit] * TEXT, (SLOT[unit] + 1) * TEXT), slice(n * LW, (n + 1) * LW)
                    gy[at] = gy[at] + rs_in[i]
                    if s < steps(n, right):
                        rs(n, right, s + 1).start()

    def gcopy(c):
        return rcopy(gxs.at[c, 1], gc_in.at[c], gc_ss.at[c], gc_rs.at[c], other)

    def image_sums(c):
        at = slice(c * CC, (c + 1) * CC)
        for b in range(2):
            rows = slice(b * S // 2, (b + 1) * S // 2)
            g = dot3(d_hi[:, rows], d_lo[:, rows], yb_hi[:, at], yb_lo[:, at], 0, 0)
            for i in range(NL):
                r = ORDER[b * 2 + i // 2]
                for j in range(NX):
                    gxs[c, i % 2, j, r] = g[i * GROUP + j * SHARE : i * GROUP + (j + 1) * SHARE, :]
        gcopy(c).start()

    def ahead(d):
        return lax.rem(x + d, NX)

    def xa(c, right):
        b = 0 if right else 1
        i = c * 2 + b
        src = gxs.at[c, 0, ahead(2), pl.ds(b * 2, 2)]
        return rcopy(src, xa_in.at[i], xa_ss.at[i], xa_rs.at[i], at_x(1 if right else NX - 1))

    def xf(c, right):
        d = 1 if right else NX - 1
        i = c * 2 + (0 if right else 1)
        return rcopy(gxs.at[c, 0, ahead(d)], xf_in.at[i], xf_ss.at[i], xf_rs.at[i], at_x(d))

    def core_done(c):
        gcopy(c).wait()
        for j in range(NX):
            gxs[c, 0, j] = gxs[c, 0, j] + gc_in[c, j]
        for right in (True, False):
            xa(c, right).start()

    def xa_done(c):
        for right in (True, False):
            xa(c, right).wait()
            d = 1 if right else NX - 1
            b = 0 if right else 1
            for i in range(2):
                r = b * 2 + i
                gxs[c, 0, ahead(d), r] = gxs[c, 0, ahead(d), r] + xa_in[c * 2 + b, i]
            xf(c, right).start()

    def q(c, r):
        i = c * 3 + r - 1
        return rcopy(zs.at[c, r], zr.at[c, r - 1], q_ss.at[i], q_rs.at[i], at_line(r))

    def xf_done(c):
        for right in (True, False):
            xf(c, right).wait()
        zs[c] = gxs[c, 0, x] + xf_in[c * 2] + xf_in[c * 2 + 1]
        for r in (2, 1, 3):
            q(c, r).start()

    image_sums(0)
    image_sums(1)
    text_sums(1)
    rs_start()
    core_done(0)
    image_sums(2)
    core_done(1)
    text_sums(0)
    lz[z] = lsum(ly, lcopies, NY)
    lcopies = lsend(lz, z, lz_ss, lz_rs, lambda d: at_z(z + d), NZ)
    core_done(2)
    xa_done(0)
    rs_take(1)
    xa_done(1)
    xa_done(2)
    rs_take(2)
    lc[k] = lsum(lz, lcopies, NZ)
    lcopies = lsend(lc, k, lc_ss, lc_rs, lambda d: other, 2)
    xf_done(0)
    lx[x] = lsum(lc, lcopies, 2)
    lcopies = lsend(lx, x, lx_ss, lx_rs, at_x, NX)
    xf_done(1)
    rs_take(3)
    xf_done(2)
    rs_take(4)
    gz[0] = gy[SLOT[0] * TEXT : SLOT[0] * TEXT + SHARE, :]
    gz[1] = gy[SLOT[0] * TEXT + SHARE : (SLOT[0] + 1) * TEXT, :]
    hcopy = rcopy(gz.at[1 - zh], gz_in, h_ss, h_rs, at_z(z + NL))
    hcopy.start()
    loss = lsum(lx, lcopies, NX) * (1.0 / (float(N) * float(N)))
    loss_o[0] = loss[0, 0]

    for c in range(NC):
        for r in range(1, NL):
            q(c, r).wait()
        gx[:, c * CC : (c + 1) * CC] = zs[c, 0] + zr[c, 0] + zr[c, 1] + zr[c, 2]
    g = scale1 * (gx[...] - y_own)
    g_o[0] = inv_x * (g - x_own * jnp.sum(x_own * g, axis=-1, keepdims=True))

    hcopy.wait()
    g = scale1 * (gz[zh] + gz_in[...] - x_own)
    g_o[1] = iy_own * (g - y_own * jnp.sum(y_own * g, axis=-1, keepdims=True))

    rcopy(gy.at[sent, :], gy.at[sent, :], rs_ss, rs_rs.at[0], other).wait_send()


def local(image, text, log_temp, bias):
    vmem = pl.BlockSpec(memory_space=pltpu.VMEM)
    smem = pl.BlockSpec(memory_space=pltpu.SMEM)
    hbm = pl.BlockSpec(memory_space=pl.ANY)
    dma = pltpu.SemaphoreType.DMA
    scratch = [
        pltpu.VMEM((BLOCK, D), F32),
        pltpu.VMEM((TEXT, D), F32),
        pltpu.VMEM((2, GROUP, D), F32),
        pltpu.VMEM((TEXT, D), F32),
        pltpu.VMEM((NL - 1, GROUP, D), F32),
        pltpu.VMEM((NL, GROUP, D), F32),
        pltpu.VMEM((T, D), F32),
        pltpu.VMEM((S, D), BF16),
        pltpu.VMEM((S, D), BF16),
        pltpu.VMEM((T, D), BF16),
        pltpu.VMEM((T, D), BF16),
        pltpu.VMEM((T, S), BF16),
        pltpu.VMEM((T, S), BF16),
        pltpu.VMEM((T, D), F32),
        pltpu.VMEM((8 * LANES, TEXT, LW), F32),
        pltpu.VMEM((2, SHARE, D), F32),
        pltpu.VMEM((SHARE, D), F32),
        pltpu.VMEM((NC, 2, NX, NL, SHARE, CC), F32),
        pltpu.VMEM((NC, NX, NL, SHARE, CC), F32),
        pltpu.VMEM((2 * NC, 2, SHARE, CC), F32),
        pltpu.VMEM((2 * NC, NL, SHARE, CC), F32),
        pltpu.VMEM((NC, NL, SHARE, CC), F32),
        pltpu.VMEM((NC, NL - 1, SHARE, CC), F32),
        pltpu.VMEM((SHARE, D), F32),
        pltpu.VMEM((8, S // 2), F32),
        pltpu.VMEM((2, 8, 128), F32),
        pltpu.VMEM((NX, 8, 128), F32),
        pltpu.VMEM((NY, 8, 128), F32),
        pltpu.VMEM((NZ, 8, 128), F32),
        dma((2,)),
    ]
    scratch += [dma, dma((8 * LANES,))]
    for n in (10, 3, 6):
        scratch += [dma((n,)), dma((n,))]
    scratch += [dma, dma((8 * LANES,))]
    for n in (NC, 2 * NC, 2 * NC, 3 * NC):
        scratch += [dma((n,)), dma((n,))]
    scratch += [dma, dma]
    for n in (1, NX - 1, NY - 1, NZ - 1):
        scratch += [dma((n,)), dma((n,))]
    loss, g = pl.pallas_call(
        kernel,
        out_shape=(
            jax.ShapeDtypeStruct((1,), F32),
            jax.ShapeDtypeStruct((2, SHARE, D), F32),
        ),
        in_specs=[hbm, hbm, smem, smem],
        out_specs=(smem, vmem),
        scratch_shapes=scratch,
        compiler_params=pltpu.CompilerParams(
            collective_id=0, has_side_effects=True, vmem_limit_bytes=56 << 20
        ),
    )(image, text, log_temp, bias)
    return loss[0], g[0], g[1]


def solution(mesh):
    in_specs = (P("dp", None), P("dp", None), P(), P())
    out_specs = (P(), P(("dp", "split"), None), P(("dp", "split"), None))
    return jax.shard_map(local, mesh=mesh, in_specs=in_specs, out_specs=out_specs, check_vma=False)
```
